32 devices in a mesh: dp: 16 (over z, x, core), tensor: 2 (over y).
Axes of the slice: x: 2, y: 2, z: 4, core: 2. Of those that a mesh axis runs over, the one named last changes fastest.
Arguments:
- inputs: bfloat16 [16384, 1024], P(('dp', 'tensor')), may hold values from -6 to 6
- grad_out: bfloat16 [16384, 1024], P(('dp', 'tensor')), may hold values from -6 to 6
- w_query: bfloat16 [1024, 2048], P('dp', 'tensor'), may hold values from -0.1875 to 0.1875
- key_weight: bfloat16 [1024, 1024], P('dp', 'tensor'), may hold values from -0.1875 to 0.1875
- value_weight: bfloat16 [1024, 1024], P('dp', 'tensor'), may hold values from -0.1875 to 0.1875
- w_output: bfloat16 [2048, 1024], P('tensor', 'dp'), may hold values from -1.5 to 1.5
- w_gate: bfloat16 [1024, 3072], P('dp', 'tensor'), may hold values from -0.1875 to 0.1875
- w_up: bfloat16 [1024, 3072], P('dp', 'tensor'), may hold values from -0.1875 to 0.1875
- w_down: bfloat16 [3072, 1024], P('tensor', 'dp'), may hold values from -0.109375 to 0.109375
- gain_attn: float32 [1024], replicated, may hold values from 0.5 to 1.5
- gain_mlp: float32 [1024], replicated, may hold values from 0.5 to 1.5
- gain_query: float32 [128], replicated, may hold values from 0.25 to 1.75
- gain_keys: float32 [128], replicated, may hold values from 0.25 to 1.75
Outputs:
- layer_out: bfloat16 [16384, 1024], P(('dp', 'tensor'))
- grad_inputs: bfloat16 [16384, 1024], P(('dp', 'tensor'))
- grad_w_query: float32 [1024, 2048], P('dp', 'tensor')
- grad_w_keys: float32 [1024, 1024], P('dp', 'tensor')
- grad_w_values: float32 [1024, 1024], P('dp', 'tensor')
- grad_w_output: float32 [2048, 1024], P('tensor', 'dp')
- grad_w_gate: float32 [1024, 3072], P('dp', 'tensor')
- grad_w_up: float32 [1024, 3072], P('dp', 'tensor')
- grad_w_down: float32 [3072, 1024], P('tensor', 'dp')
- grad_gain_attn: float32 [1024], replicated
- grad_gain_mlp: float32 [1024], replicated
- grad_gain_query: float32 [128], replicated
- grad_gain_keys: float32 [128], replicated
The draws below stay inside these ranges and needn't reach their ends.
All inputs are finite; a program needn't handle non-finite values.
Results may differ from the reference program's by a relative error of at most 0.018.
Values may be sent and summed in bfloat16 or wider, within the bound.
No kernel may reach another device: no remote copies, remote signals or barrier semaphores. Data moves between devices by JAX's collectives and lax.ppermute only.
A program may use at most 192 MiB of HBM per device.

```python
import jax
import jax.numpy as jnp
from jax import lax

MODEL_WIDTH = 1024
QUERY_HEAD_COUNT = 16
KV_HEAD_COUNT = 8
HEAD_SIZE = 128
FF = 3072
SEQUENCE_TOKENS = 512
SEQS_DEV = 2
TOKENS = 16384


def block_scale(own_key, dims, cuts, low, high):
    def one(position, shards_of):
        heights = jax.random.uniform(jax.random.fold_in(jax.random.fold_in(own_key, 6), position), (shards_of,), jnp.float32, low / len(cuts), high / len(cuts))
        return jnp.repeat(jnp.exp(heights), dims[position] // shards_of).reshape((-1,) + (1,) * (len(dims) - position - 1))

    gain = one(*cuts[0])
    for cut in cuts[1:]:
        gain = gain * one(*cut)
    return gain


def noise(stream_key, dims, width, limit, cuts=(), kind=jnp.bfloat16):
    gain = block_scale(stream_key, dims, cuts, -0.22, 0.18) if cuts else 1.0
    values = jax.random.normal(stream_key, dims, jnp.float32) * width * gain
    return jnp.minimum(jnp.maximum(values, -limit), limit).astype(kind)


def setup_inputs(seed: int = 0) -> dict:
    arg_keys = jax.random.split(jax.random.key(seed), 14)
    return {
        "inputs": noise(arg_keys[0], (TOKENS, MODEL_WIDTH), 1.0, 6.0, ((0, 32),)),
        "grad_out": noise(arg_keys[1], (TOKENS, MODEL_WIDTH), 1.0, 6.0, ((0, 32),)),
        "w_query": noise(arg_keys[2], (MODEL_WIDTH, QUERY_HEAD_COUNT * HEAD_SIZE), MODEL_WIDTH ** -0.5, 0.1875, ((0, 16), (1, 2))),
        "key_weight": noise(arg_keys[3], (MODEL_WIDTH, KV_HEAD_COUNT * HEAD_SIZE), MODEL_WIDTH ** -0.5, 0.1875, ((0, 16), (1, 2))),
        "value_weight": noise(arg_keys[4], (MODEL_WIDTH, KV_HEAD_COUNT * HEAD_SIZE), MODEL_WIDTH ** -0.5, 0.1875, ((0, 16), (1, 2))),
        "w_output": noise(arg_keys[5], (QUERY_HEAD_COUNT * HEAD_SIZE, MODEL_WIDTH), (QUERY_HEAD_COUNT * HEAD_SIZE * 4 // SEQUENCE_TOKENS) ** -0.5, 1.5, ((0, 2), (1, 16))),
        "w_gate": noise(arg_keys[6], (MODEL_WIDTH, FF), MODEL_WIDTH ** -0.5, 0.1875, ((0, 16), (1, 2))),
        "w_up": noise(arg_keys[7], (MODEL_WIDTH, FF), MODEL_WIDTH ** -0.5, 0.1875, ((0, 16), (1, 2))),
        "w_down": noise(arg_keys[8], (FF, MODEL_WIDTH), FF ** -0.5, 0.109375, ((0, 2), (1, 16))),
        "gain_attn": jnp.clip(1.0 + 0.1 * jax.random.normal(arg_keys[9], (MODEL_WIDTH,), jnp.float32), 0.5, 1.5),
        "gain_mlp": jnp.clip(1.0 + 0.1 * jax.random.normal(arg_keys[10], (MODEL_WIDTH,), jnp.float32), 0.5, 1.5),
        "gain_query": jnp.clip(1.0 + 0.15 * jax.random.normal(arg_keys[11], (HEAD_SIZE,), jnp.float32), 0.25, 1.75),
        "gain_keys": jnp.clip(1.0 + 0.15 * jax.random.normal(arg_keys[12], (HEAD_SIZE,), jnp.float32), 0.25, 1.75),
    }


EPSILON = 1e-06
THETA = 1000000.0
TOP_PRECISION = lax.Precision.HIGHEST

@jax.custom_vjp
def reduced_precision(v):
    return lax.optimization_barrier(v.astype(jnp.bfloat16)).astype(jnp.float32)

@jax.custom_vjp
def reduced_backward(v):
    return v

def low_keep(v):
    return (reduced_precision(v), None)

def low_pass(kept, grad):
    return (grad,)

def back_keep(v):
    return (v, None)

def back_low(kept, grad):
    return (reduced_precision(grad),)
reduced_precision.defvjp(low_keep, low_pass)
reduced_backward.defvjp(back_keep, back_low)

def row_norm(values, norm_gain):
    return values * lax.rsqrt(lax.optimization_barrier(jnp.mean(values * values, axis=-1, keepdims=True)) + EPSILON) * norm_gain

def rotary(values):
    length = values.shape[1]
    half_width = values.shape[-1] // 2
    places = jnp.arange(length, dtype=jnp.float32)
    inverse = THETA ** (-2.0 * jnp.arange(half_width, dtype=jnp.float32) / values.shape[-1])
    angles = places[:, None] * inverse[None, :]
    cosine = jnp.concatenate([jnp.cos(angles), jnp.cos(angles)], axis=-1)[:, None, :]
    sine = jnp.concatenate([jnp.sin(angles), jnp.sin(angles)], axis=-1)[:, None, :]
    turned = jnp.concatenate([-values[..., half_width:], values[..., :half_width]], axis=-1)
    return values * cosine + turned * sine

def layer(inputs, w_query, key_weight, value_weight, w_output, w_gate, w_up, w_down, gain_attn, gain_mlp, gain_query, gain_keys):
    total_rows = inputs.shape[0]
    sequence_batch = total_rows // SEQUENCE_TOKENS
    normalized_rows = reduced_precision(row_norm(inputs, gain_attn))
    queries = reduced_backward(jnp.dot(normalized_rows, w_query, precision=TOP_PRECISION)).reshape(sequence_batch, SEQUENCE_TOKENS, QUERY_HEAD_COUNT, HEAD_SIZE)
    unrotated_keys = reduced_backward(jnp.dot(normalized_rows, key_weight, precision=TOP_PRECISION)).reshape(sequence_batch, SEQUENCE_TOKENS, KV_HEAD_COUNT, HEAD_SIZE)
    projected_values = reduced_precision(reduced_backward(jnp.dot(normalized_rows, value_weight, precision=TOP_PRECISION))).reshape(sequence_batch, SEQUENCE_TOKENS, KV_HEAD_COUNT, HEAD_SIZE)
    queries_rot = reduced_precision(rotary(row_norm(queries, gain_query)))
    keys_rot = reduced_precision(rotary(row_norm(unrotated_keys, gain_keys)))
    grouped_heads = QUERY_HEAD_COUNT // KV_HEAD_COUNT
    keys_all = jnp.repeat(keys_rot, grouped_heads, axis=2)
    values_all = jnp.repeat(projected_values, grouped_heads, axis=2)
    scores = reduced_backward(jnp.einsum('bqhd,bkhd->bhqk', queries_rot, keys_all, precision=TOP_PRECISION) * HEAD_SIZE ** (-0.5))
    places = jnp.arange(SEQUENCE_TOKENS)
    scores = jnp.where(places[:, None] >= places[None, :], scores, -1e+30)
    largest = lax.optimization_barrier(jnp.max(scores, axis=-1, keepdims=True))
    exponents = jnp.exp(scores - largest)
    attn_probs = reduced_precision(exponents / lax.optimization_barrier(jnp.sum(exponents, axis=-1, keepdims=True)))
    head_out = reduced_precision(reduced_backward(jnp.einsum('bhqk,bkhd->bqhd', attn_probs, values_all, precision=TOP_PRECISION)))
    head_out = head_out.reshape(total_rows, QUERY_HEAD_COUNT * HEAD_SIZE)
    attended = reduced_backward(jnp.dot(head_out, w_output, precision=TOP_PRECISION))
    middle = inputs + attended
    normed_mlp = reduced_precision(row_norm(middle, gain_mlp))
    gate_proj = reduced_backward(jnp.dot(normed_mlp, w_gate, precision=TOP_PRECISION))
    up_proj = reduced_backward(jnp.dot(normed_mlp, w_up, precision=TOP_PRECISION))
    hidden = reduced_precision(jax.nn.silu(gate_proj) * up_proj)
    return middle + reduced_backward(jnp.dot(hidden, w_down, precision=TOP_PRECISION))

def reference(inputs, grad_out, w_query, key_weight, value_weight, w_output, w_gate, w_up, w_down, gain_attn, gain_mlp, gain_query, gain_keys):
    params = tuple((weight.astype(jnp.float32) for weight in (w_query, key_weight, value_weight, w_output, w_gate, w_up, w_down, gain_attn, gain_mlp, gain_query, gain_keys)))
    group_rows = SEQS_DEV * SEQUENCE_TOKENS
    blocks = inputs.shape[0] // group_rows
    stacked_in = inputs.astype(jnp.float32).reshape(blocks, group_rows, MODEL_WIDTH)
    stacked_grad = grad_out.astype(jnp.float32).reshape(blocks, group_rows, MODEL_WIDTH)

    def accumulate(running, block_pair):
        block_in, block_grad = block_pair
        result, pullback = jax.vjp(layer, block_in, *params)
        gradients = pullback(block_grad)
        running = tuple((before + gradient for before, gradient in zip(running, gradients[1:])))
        return (running, (result.astype(jnp.bfloat16), gradients[0].astype(jnp.bfloat16)))
    start = tuple((jnp.zeros_like(weight) for weight in params))
    running, (results, grad_blocks) = lax.scan(accumulate, start, (stacked_in, stacked_grad))
    return (results.reshape(-1, MODEL_WIDTH), grad_blocks.reshape(-1, MODEL_WIDTH), running[0], running[1], running[2], running[3], running[4], running[5], running[6], running[7], running[8], running[9], running[10])
```

```python
import functools

import jax
import jax.numpy as jnp
import numpy as np
from jax import lax
from jax.experimental import pallas as pl
from jax.experimental.pallas import tpu as pltpu
from jax.sharding import PartitionSpec as P

SEQ = 512
EPSILON = 1e-06
THETA = 1000000.0
F32 = jnp.float32
BF16 = jnp.bfloat16
VMEM_LIMIT = 56 * 1024 * 1024


def dot(left, right):
    return lax.dot_general(left, right, (((1,), (0,)), ((), ())), preferred_element_type=F32)


def dot_t(left, right):
    return lax.dot_general(left, right, (((1,), (1,)), ((), ())), preferred_element_type=F32)


def rope_tables(width):
    half = width // 2
    places = np.arange(SEQ, dtype=np.float32)
    inverse = (THETA ** (-2.0 * np.arange(half, dtype=np.float32) / width)).astype(np.float32)
    angles = places[:, None] * inverse[None, :]
    cosine = np.concatenate([np.cos(angles), np.cos(angles)], axis=-1)
    sine = np.concatenate([-np.sin(angles), np.sin(angles)], axis=-1)
    return cosine.astype(np.float32), sine.astype(np.float32)


def rope(values, cosine, sine):
    half = values.shape[-1] // 2
    return values * cosine + pltpu.roll(values, half, 1) * sine


def rope_back(values, cosine, sine):
    half = values.shape[-1] // 2
    return values * cosine + pltpu.roll(values * sine, half, 1)


def exponents_t(keys_rot, query_rot, factor):
    scores = dot_t(keys_rot, query_rot)
    key_place = lax.broadcasted_iota(jnp.int32, scores.shape, 0)
    query_place = lax.broadcasted_iota(jnp.int32, scores.shape, 1)
    return jnp.where(key_place <= query_place, jnp.exp2(scores * factor), 0.0)


def attend_kernel(
    group, width, normed_ref, weight_ref, cos_ref, sin_ref, gain_q_ref, gain_k_ref, part_ref, kept_ref, total
):
    step = pl.program_id(0)
    rows = normed_ref.shape[0]
    wide = group * width
    factor = float(width**-0.5 * np.log2(np.e))
    proj = dot(normed_ref[...], weight_ref[:, : wide + 2 * width])
    kept_ref[:, : wide + width] = proj[:, : wide + width].astype(BF16)
    values = proj[:, wide + width :].astype(BF16)
    base = 2 * (wide + width)
    kept_ref[:, base : base + width] = values
    for seq in range(rows // SEQ):
        place = slice(seq * SEQ, (seq + 1) * SEQ)
        rotated = []
        for head in range(group + 1):
            raw = proj[place, head * width : (head + 1) * width]
            scale = lax.rsqrt(jnp.mean(raw * raw, axis=-1, keepdims=True) + EPSILON)
            gain = gain_q_ref[...] if head < group else gain_k_ref[...]
            turned = rope(raw * scale * gain, cos_ref[...], sin_ref[...]).astype(BF16)
            kept_ref[place, wide + width + head * width : wide + width + (head + 1) * width] = turned
            rotated.append(turned)
        values_t = values[place].T
        for head in range(group):
            exponents = exponents_t(rotated[group], rotated[head], factor)
            sums = jnp.sum(exponents, axis=0, keepdims=True)
            out_t = dot(values_t, exponents.astype(BF16)) * (1.0 / sums)
            start = base + width + head * width
            kept_ref[place, start : start + width] = out_t.T.astype(BF16)
    out = dot_t(kept_ref[:, base + width :], weight_ref[:, wide + 2 * width :])

    @pl.when(step == 0)
    def _():
        total[...] = out

    @pl.when(step > 0)
    def _():
        total[...] += out

    @pl.when(step == pl.num_programs(0) - 1)
    def _():
        part_ref[...] = total[...].astype(BF16)


def attend(normed, weights, tables, gain_q, gain_k, heads, group, width):
    rows, model = normed.shape
    block = weights.shape[1] // heads
    kept_block = (4 * group + 3) * width - group * width
    whole = lambda *dims: pl.BlockSpec(dims, lambda j: (0,) * len(dims))
    flops = heads * (2 * rows * model * block + 4 * rows * SEQ * group * width)
    return pl.pallas_call(
        functools.partial(attend_kernel, group, width),
        grid=(heads,),
        in_specs=[
            whole(rows, model),
            pl.BlockSpec((model, block), lambda j: (0, j)),
            whole(SEQ, width),
            whole(SEQ, width),
            whole(1, width),
            whole(1, width),
        ],
        out_specs=[whole(rows, model), pl.BlockSpec((rows, kept_block), lambda j: (0, j))],
        out_shape=[
            jax.ShapeDtypeStruct((rows, model), BF16),
            jax.ShapeDtypeStruct((rows, heads * kept_block), BF16),
        ],
        scratch_shapes=[pltpu.VMEM((rows, model), F32)],
        compiler_params=pltpu.CompilerParams(vmem_limit_bytes=VMEM_LIMIT),
        cost_estimate=pl.CostEstimate(
            flops=flops, bytes_accessed=weights.size * 2 + 4 * rows * model * 2, transcendentals=0
        ),
        name="attend",
    )(normed, weights, *tables, gain_q, gain_k)


def mlp_kernel(
    normed_ref,
    grad_ref,
    weight_ref,
    gain_ref,
    out_ref,
    dx_ref,
    dw_ref,
    dgain_ref,
    normed_t,
    grad_t,
    out_total,
    dx_total,
):
    step = pl.program_id(0)
    units = weight_ref.shape[1] // 3

    @pl.when(step == 0)
    def _():
        normed_t[...] = normed_ref[...].T
        grad_t[...] = grad_ref[...].T
        out_total[...] = jnp.zeros_like(out_total)
        dx_total[...] = jnp.zeros_like(dx_total)

    both = dot(normed_ref[...], weight_ref[:, : 2 * units])
    gate, up = both[:, :units], both[:, units:]
    sig = 1.0 / (1.0 + jnp.exp(-gate))
    silu = gate * sig
    hidden = (silu * up).astype(BF16)
    grad_hidden = dot(grad_ref[...], weight_ref[:, 2 * units :])
    grad_gate = (grad_hidden * up * (sig + silu * (1.0 - sig))).astype(BF16)
    grad_up = (grad_hidden * silu).astype(BF16)
    out_total[...] += dot_t(hidden, weight_ref[:, 2 * units :])
    dx_total[...] += dot_t(grad_gate, weight_ref[:, :units]) + dot_t(
        grad_up, weight_ref[:, units : 2 * units]
    )
    dw_ref[:, :units] = dot(normed_t[...], grad_gate).astype(BF16)
    dw_ref[:, units : 2 * units] = dot(normed_t[...], grad_up).astype(BF16)
    dw_ref[:, 2 * units :] = dot(grad_t[...], hidden).astype(BF16)

    @pl.when(step == pl.num_programs(0) - 1)
    def _():
        out_ref[...] = out_total[...].astype(BF16)
        dx_ref[...] = dx_total[...].astype(BF16)
        dgain_ref[...] = (
            jnp.sum(normed_ref[...].astype(F32) * dx_total[...], axis=0, keepdims=True) / gain_ref[...]
        )


def mlp(normed, grad_rows, weights, gain, steps):
    rows, model = normed.shape
    block = weights.shape[1] // steps
    whole = lambda *dims: pl.BlockSpec(dims, lambda j: (0,) * len(dims))
    columns = pl.BlockSpec((model, block), lambda j: (0, j))
    return pl.pallas_call(
        mlp_kernel,
        grid=(steps,),
        in_specs=[whole(rows, model), whole(rows, model), columns, whole(1, model)],
        out_specs=[whole(rows, model), whole(rows, model), columns, whole(1, model)],
        out_shape=[
            jax.ShapeDtypeStruct((rows, model), BF16),
            jax.ShapeDtypeStruct((rows, model), BF16),
            jax.ShapeDtypeStruct(weights.shape, BF16),
            jax.ShapeDtypeStruct((1, model), F32),
        ],
        scratch_shapes=[
            pltpu.VMEM((model, rows), BF16),
            pltpu.VMEM((model, rows), BF16),
            pltpu.VMEM((rows, model), F32),
            pltpu.VMEM((rows, model), F32),
        ],
        compiler_params=pltpu.CompilerParams(vmem_limit_bytes=VMEM_LIMIT),
        cost_estimate=pl.CostEstimate(
            flops=6 * rows * weights.size, bytes_accessed=4 * weights.size + 8 * rows * model, transcendentals=0
        ),
        name="mlp",
    )(normed, grad_rows, weights, gain)


def attend_back_kernel(
    group,
    width,
    normed_ref,
    grad_ref,
    weight_ref,
    kept_ref,
    cos_ref,
    sin_ref,
    gain_q_ref,
    gain_k_ref,
    gain_ref,
    dx_ref,
    dw_ref,
    dgain_ref,
    dgain_heads_ref,
    normed_t,
    grad_t,
    dx_total,
    dproj,
):
    step = pl.program_id(0)
    rows = normed_ref.shape[0]
    wide = group * width
    scaling = float(width**-0.5)
    factor = float(width**-0.5 * np.log2(np.e))
    rot = wide + width
    base = 2 * rot

    @pl.when(step == 0)
    def _():
        normed_t[...] = normed_ref[...].T
        grad_t[...] = grad_ref[...].T
        dx_total[...] = jnp.zeros_like(dx_total)
        dgain_heads_ref[...] = jnp.zeros_like(dgain_heads_ref)

    grad_heads = dot(grad_ref[...], weight_ref[:, wide + 2 * width :]).astype(BF16)
    dw_ref[:, wide + 2 * width :] = dot(grad_t[...], kept_ref[:, base + width :]).astype(BF16)

    def head_back(place, head, cotangent):
        gain = gain_q_ref[...] if head < group else gain_k_ref[...]
        raw = kept_ref[place, head * width : (head + 1) * width].astype(F32)
        scale = lax.rsqrt(jnp.mean(raw * raw, axis=-1, keepdims=True) + EPSILON)
        unit = raw * scale
        cot = rope_back(cotangent * scaling, cos_ref[...], sin_ref[...])
        row = 0 if head < group else 1
        dgain_heads_ref[row : row + 1, :] += jnp.sum(cot * unit, axis=0, keepdims=True)
        cot = cot * gain
        grad = scale * (cot - unit * jnp.mean(unit * cot, axis=-1, keepdims=True))
        dproj[place, head * width : (head + 1) * width] = grad.astype(BF16)

    for seq in range(rows // SEQ):
        place = slice(seq * SEQ, (seq + 1) * SEQ)
        keys_rot = kept_ref[place, rot + wide : rot + wide + width]
        keys_t = keys_rot.T
        values = kept_ref[place, base : base + width]
        dkeys = jnp.zeros((SEQ, width), F32)
        dvalues = jnp.zeros((SEQ, width), F32)
        for head in range(group):
            query_rot = kept_ref[place, rot + head * width : rot + (head + 1) * width]
            grad_head = grad_heads[place, head * width : (head + 1) * width]
            exponents = exponents_t(keys_rot, query_rot, factor)
            probs = exponents * (1.0 / jnp.sum(exponents, axis=0, keepdims=True))
            dprobs = dot_t(values, grad_head)
            inner = jnp.sum(probs * dprobs, axis=0, keepdims=True)
            dscores = (probs * (dprobs - inner)).astype(BF16)
            dvalues += dot(probs.astype(BF16), grad_head)
            dkeys += dot(dscores, query_rot)
            head_back(place, head, dot(keys_t, dscores).T)
        head_back(place, group, dkeys)
        dproj[place, wide + width :] = dvalues.astype(BF16)

    dx_total[...] += dot_t(dproj[...], weight_ref[:, : wide + 2 * width])
    dw_ref[:, : wide + 2 * width] = dot(normed_t[...], dproj[...]).astype(BF16)

    @pl.when(step == pl.num_programs(0) - 1)
    def _():
        dx_ref[...] = dx_total[...].astype(BF16)
        dgain_ref[...] = (
            jnp.sum(normed_ref[...].astype(F32) * dx_total[...], axis=0, keepdims=True) / gain_ref[...]
        )


def attend_back(normed, grad_rows, weights, kept, tables, gain_q, gain_k, gain, heads, group, width):
    rows, model = normed.shape
    block = weights.shape[1] // heads
    kept_block = kept.shape[1] // heads
    whole = lambda *dims: pl.BlockSpec(dims, lambda j: (0,) * len(dims))
    columns = pl.BlockSpec((model, block), lambda j: (0, j))
    flops = heads * (4 * rows * model * block + 10 * rows * SEQ * group * width)
    return pl.pallas_call(
        functools.partial(attend_back_kernel, group, width),
        grid=(heads,),
        in_specs=[
            whole(rows, model),
            whole(rows, model),
            columns,
            pl.BlockSpec((rows, kept_block), lambda j: (0, j)),
            whole(SEQ, width),
            whole(SEQ, width),
            whole(1, width),
            whole(1, width),
            whole(1, model),
        ],
        out_specs=[whole(rows, model), columns, whole(1, model), whole(8, width)],
        out_shape=[
            jax.ShapeDtypeStruct((rows, model), BF16),
            jax.ShapeDtypeStruct(weights.shape, BF16),
            jax.ShapeDtypeStruct((1, model), F32),
            jax.ShapeDtypeStruct((8, width), F32),
        ],
        scratch_shapes=[
            pltpu.VMEM((model, rows), BF16),
            pltpu.VMEM((model, rows), BF16),
            pltpu.VMEM((rows, model), F32),
            pltpu.VMEM((rows, (group + 2) * width), BF16),
        ],
        compiler_params=pltpu.CompilerParams(vmem_limit_bytes=VMEM_LIMIT),
        cost_estimate=pl.CostEstimate(
            flops=flops, bytes_accessed=4 * weights.size + 10 * rows * model, transcendentals=0
        ),
        name="attend_back",
    )(normed, grad_rows, weights, kept, *tables, gain_q, gain_k, gain)


def unit_rows(values):
    scale = lax.rsqrt(jnp.mean(values * values, axis=-1, keepdims=True) + EPSILON)
    return values * scale, scale


def norm_back(unit, scale, cotangent):
    return scale * (cotangent - unit * jnp.mean(unit * cotangent, axis=-1, keepdims=True))


def pack(parts, pieces):
    rows = parts[0].shape[0]
    split = [part.reshape(rows, pieces, part.shape[1] // pieces) for part in parts]
    return jnp.concatenate(split, axis=2).reshape(rows, -1)


def unpack(packed, pieces, widths):
    rows = packed.shape[0]
    split = packed.reshape(rows, pieces, -1).astype(F32)
    ends = np.cumsum([width // pieces for width in widths])
    return [
        split[:, :, end - width // pieces : end].reshape(rows, width) for end, width in zip(ends, widths)
    ]


def body(
    tensor_size,
    inputs,
    grad_out,
    w_query,
    key_weight,
    value_weight,
    w_output,
    w_gate,
    w_up,
    w_down,
    gain_attn,
    gain_mlp,
    gain_query,
    gain_keys,
):
    rows = inputs.shape[0]
    width = gain_query.shape[0]
    heads = key_weight.shape[1] // width
    group = w_query.shape[1] // key_weight.shape[1]
    hidden = w_gate.shape[1]
    steps = max(1, hidden // 256)
    by_pair = tensor_size == 2 and rows % SEQ == 0
    swap = ((0, 1), (1, 0))

    def gather_rows(own):
        if by_pair:
            return jnp.concatenate([own, lax.ppermute(own, "tensor", swap)], axis=0)
        return lax.all_gather(own, "tensor", axis=0, tiled=True)

    def sum_rows(part):
        if by_pair:
            return part[:rows].astype(F32) + lax.ppermute(part[rows:], "tensor", swap).astype(F32)
        return lax.psum_scatter(part, "tensor", scatter_dimension=0, tiled=True).astype(F32)

    tables = rope_tables(width)
    gain_q, gain_k = gain_query[None, :], gain_keys[None, :]
    attn_weights = lax.all_gather(
        pack([w_query, key_weight, value_weight, w_output.T], heads), "dp", axis=0, tiled=True
    )
    mlp_weights = lax.all_gather(pack([w_gate, w_up, w_down.T], steps), "dp", axis=0, tiled=True)

    inputs_f = inputs.astype(F32)
    unit_in, scale_in = unit_rows(inputs_f)
    normed = gather_rows((unit_in * gain_attn).astype(BF16))
    grad_rows = gather_rows(grad_out)
    part, kept = attend(normed, attn_weights, tables, gain_q, gain_k, heads, group, width)
    middle = inputs_f + sum_rows(part)
    unit_mid, scale_mid = unit_rows(middle)
    normed_mlp = gather_rows((unit_mid * gain_mlp).astype(BF16))
    ffn_part, dx_part, dw_mlp, dgain_mlp = mlp(normed_mlp, grad_rows, mlp_weights, gain_mlp[None, :], steps)
    grad_normed_mlp = sum_rows(dx_part)
    grad_middle = grad_out.astype(F32) + norm_back(unit_mid, scale_mid, grad_normed_mlp * gain_mlp)
    grad_attended = gather_rows(grad_middle.astype(BF16))
    layer_out = (middle + sum_rows(ffn_part)).astype(BF16)
    mlp_grads = lax.psum_scatter(dw_mlp, "dp", scatter_dimension=0, tiled=True)
    dx_part, dw_attn, dgain_attn, dgain_heads = attend_back(
        normed, grad_attended, attn_weights, kept, tables, gain_q, gain_k, gain_attn[None, :], heads, group, width
    )
    attn_grads = lax.psum_scatter(dw_attn, "dp", scatter_dimension=0, tiled=True)
    gains = lax.psum(
        jnp.concatenate([dgain_attn[0], dgain_mlp[0], dgain_heads[0], dgain_heads[1]]), ("dp", "tensor")
    )
    grad_normed = sum_rows(dx_part)
    grad_inputs = (grad_middle + norm_back(unit_in, scale_in, grad_normed * gain_attn)).astype(BF16)

    model = inputs.shape[1]
    query_part, keys_part, values_part, output_part = unpack(
        attn_grads, heads, [w_query.shape[1], key_weight.shape[1], value_weight.shape[1], w_output.shape[0]]
    )
    gate_part, up_part, down_part = unpack(mlp_grads, steps, [hidden, hidden, hidden])
    return (
        layer_out,
        grad_inputs,
        query_part,
        keys_part,
        values_part,
        output_part.T,
        gate_part,
        up_part,
        down_part.T,
        gains[:model],
        gains[model : 2 * model],
        gains[2 * model : 2 * model + width],
        gains[2 * model + width :],
    )


def solution(mesh):
    rows = P(("dp", "tensor"), None)
    wide, tall = P("dp", "tensor"), P("tensor", "dp")
    return jax.shard_map(
        functools.partial(body, mesh.shape["tensor"]),
        mesh=mesh,
        in_specs=(rows, rows, wide, wide, wide, tall, wide, wide, tall, P(), P(), P(), P()),
        out_specs=(rows, rows, wide, wide, wide, tall, wide, wide, tall, P(), P(), P(), P()),
        check_vma=False,
    )
```

```python
import functools

import jax
import jax.numpy as jnp
import numpy as np
from jax import lax
from jax.experimental import pallas as pl
from jax.experimental.pallas import tpu as pltpu
from jax.sharding import PartitionSpec as P

SEQ = 512
EPSILON = 1e-06
THETA = 1000000.0
F32 = jnp.float32
BF16 = jnp.bfloat16
VMEM_LIMIT = 56 * 1024 * 1024


def dot(left, right):
    return lax.dot_general(left, right, (((1,), (0,)), ((), ())), preferred_element_type=F32)


def dot_t(left, right):
    return lax.dot_general(left, right, (((1,), (1,)), ((), ())), preferred_element_type=F32)


def whole(array):
    dims = array.shape
    return pl.BlockSpec(dims, lambda *_: (0,) * len(dims))


def columns(array, count, first=0):
    return pl.BlockSpec((array.shape[0], array.shape[1] // count), lambda j: (0, first + j))


def kernel_call(kernel, name, grid, inputs, outputs, scratch, flops, after=()):
    known = len(inputs)

    def run(*refs):
        kernel(*refs[:known], *refs[known + len(after) :])

    moved = sum(array.size * array.dtype.itemsize for array, _ in inputs)
    return pl.pallas_call(
        run,
        grid=grid,
        in_specs=[spec for _, spec in inputs] + [pl.BlockSpec(memory_space=pl.ANY)] * len(after),
        out_specs=[spec for _, _, spec in outputs],
        out_shape=[jax.ShapeDtypeStruct(shape, dtype) for shape, dtype, _ in outputs],
        scratch_shapes=scratch,
        compiler_params=pltpu.CompilerParams(vmem_limit_bytes=VMEM_LIMIT),
        cost_estimate=pl.CostEstimate(flops=flops, bytes_accessed=moved, transcendentals=0),
        name=name,
    )(*[array for array, _ in inputs], *after)


def rope_tables(width):
    half = width // 2
    places = np.arange(SEQ, dtype=np.float32)
    inverse = (THETA ** (-2.0 * np.arange(half, dtype=np.float32) / width)).astype(np.float32)
    angles = places[:, None] * inverse[None, :]
    cosine = np.concatenate([np.cos(angles), np.cos(angles)], axis=-1)
    sine = np.concatenate([-np.sin(angles), np.sin(angles)], axis=-1)
    return cosine.astype(np.float32), sine.astype(np.float32)


def rope(values, cosine, sine):
    half = values.shape[-1] // 2
    return values * cosine + pltpu.roll(values, half, 1) * sine


def rope_back(values, cosine, sine):
    half = values.shape[-1] // 2
    return values * cosine + pltpu.roll(values * sine, half, 1)


def exponents_t(keys_rot, query_rot, factor):
    scores = dot_t(keys_rot, query_rot)
    key_place = lax.broadcasted_iota(jnp.int32, scores.shape, 0)
    query_place = lax.broadcasted_iota(jnp.int32, scores.shape, 1)
    return jnp.where(key_place <= query_place, jnp.exp2(scores * factor), 0.0)


def attend_kernel(
    group, width, normed_ref, weight_ref, cos_ref, sin_ref, gain_q_ref, gain_k_ref, part_ref, kept_ref, total
):
    step = pl.program_id(0)
    rows = normed_ref.shape[0]
    wide = group * width
    factor = float(width**-0.5 * np.log2(np.e))
    proj = dot(normed_ref[...], weight_ref[:, : wide + 2 * width])
    kept_ref[:, : wide + width] = proj[:, : wide + width].astype(BF16)
    values = proj[:, wide + width :].astype(BF16)
    base = 2 * (wide + width)
    kept_ref[:, base : base + width] = values
    for seq in range(rows // SEQ):
        place = slice(seq * SEQ, (seq + 1) * SEQ)
        rotated = []
        for head in range(group + 1):
            raw = proj[place, head * width : (head + 1) * width]
            scale = lax.rsqrt(jnp.mean(raw * raw, axis=-1, keepdims=True) + EPSILON)
            gain = gain_q_ref[...] if head < group else gain_k_ref[...]
            turned = rope(raw * scale * gain, cos_ref[...], sin_ref[...]).astype(BF16)
            kept_ref[place, wide + width + head * width : wide + width + (head + 1) * width] = turned
            rotated.append(turned)
        values_t = values[place].T
        for head in range(group):
            exponents = exponents_t(rotated[group], rotated[head], factor)
            sums = jnp.sum(exponents, axis=0, keepdims=True)
            out_t = dot(values_t, exponents.astype(BF16)) * (1.0 / sums)
            start = base + width + head * width
            kept_ref[place, start : start + width] = out_t.T.astype(BF16)
    out = dot_t(kept_ref[:, base + width :], weight_ref[:, wide + 2 * width :])

    @pl.when(step == 0)
    def _():
        total[...] = out

    @pl.when(step > 0)
    def _():
        total[...] += out

    @pl.when(step == pl.num_programs(0) - 1)
    def _():
        part_ref[...] = total[...].astype(BF16)


def attend(normed, weights, tables, gain_q, gain_k, heads, group, width, after=()):
    rows, model = normed.shape
    block = weights.shape[1] // heads
    kept = jax.ShapeDtypeStruct((rows, heads * (3 * group + 3) * width), BF16)
    return kernel_call(
        functools.partial(attend_kernel, group, width),
        "attend",
        (heads,),
        [
            (normed, whole(normed)),
            (weights, columns(weights, heads)),
            *[(array, whole(array)) for array in (*tables, gain_q, gain_k)],
        ],
        [(normed.shape, BF16, whole(normed)), (kept.shape, BF16, columns(kept, heads))],
        [pltpu.VMEM((rows, model), F32)],
        heads * (2 * rows * model * block + 4 * rows * SEQ * group * width),
        after,
    )


def turn_kernel(places_ref, source_ref, target_ref):
    model = target_ref.shape[0]
    count = places_ref.shape[0]
    block = model // count
    for index in range(count):
        start = pl.multiple_of(places_ref[index] * block, block)
        target_ref[pl.ds(start, block), :] = source_ref[:, index * block : (index + 1) * block].T


def turn(places, source, after=()):
    target = jax.ShapeDtypeStruct(source.shape[::-1], BF16)
    return kernel_call(
        turn_kernel,
        "turn",
        (1,),
        [(places, pl.BlockSpec(memory_space=pltpu.SMEM)), (source, whole(source))],
        [(target.shape, BF16, whole(target))],
        [],
        0,
        after,
    )[0]


def mlp_kernel(normed_ref, grad_ref, weight_ref, gain_ref, out_ref, dx_ref, kept_ref, dgain_ref, out_total, dx_total):
    step = pl.program_id(0)
    units = weight_ref.shape[1] // 3

    @pl.when(step == 0)
    def _():
        out_total[...] = jnp.zeros_like(out_total)
        dx_total[...] = jnp.zeros_like(dx_total)

    both = dot(normed_ref[...], weight_ref[:, : 2 * units])
    gate, up = both[:, :units], both[:, units:]
    sig = 1.0 / (1.0 + jnp.exp(-gate))
    silu = gate * sig
    hidden = (silu * up).astype(BF16)
    grad_hidden = dot(grad_ref[...], weight_ref[:, 2 * units :])
    grad_gate = (grad_hidden * up * (sig + silu * (1.0 - sig))).astype(BF16)
    grad_up = (grad_hidden * silu).astype(BF16)
    kept_ref[:, :units] = grad_gate
    kept_ref[:, units : 2 * units] = grad_up
    kept_ref[:, 2 * units :] = hidden
    out_total[...] += dot_t(hidden, weight_ref[:, 2 * units :])
    dx_total[...] += dot_t(kept_ref[:, : 2 * units], weight_ref[:, : 2 * units])

    @pl.when(step == pl.num_programs(0) - 1)
    def _():
        out_ref[...] = out_total[...].astype(BF16)
        dx_ref[...] = dx_total[...].astype(BF16)
        dgain_ref[...] = (
            jnp.sum(normed_ref[...].astype(F32) * dx_total[...], axis=0, keepdims=True) / gain_ref[...]
        )


def mlp(normed, grad_rows, weights, gain, steps, after=()):
    rows, model = normed.shape
    kept = jax.ShapeDtypeStruct((rows, weights.shape[1]), BF16)
    return kernel_call(
        mlp_kernel,
        "mlp",
        (steps,),
        [
            (normed, whole(normed)),
            (grad_rows, whole(grad_rows)),
            (weights, columns(weights, steps)),
            (gain, whole(gain)),
        ],
        [
            (normed.shape, BF16, whole(normed)),
            (normed.shape, BF16, whole(normed)),
            (kept.shape, BF16, columns(kept, steps)),
            (gain.shape, F32, whole(gain)),
        ],
        [pltpu.VMEM((rows, model), F32), pltpu.VMEM((rows, model), F32)],
        4 * rows * weights.size,
        after,
    )


def mlp_grads_kernel(parts, *refs):
    normed_t, grad_t, kept = refs[:parts], refs[parts : 2 * parts], refs[2 * parts : 3 * parts]
    units = kept[0].shape[1] // 3
    half = normed_t[0].shape[0] // 2
    for ref, place in zip(refs[3 * parts :], (slice(0, half), slice(half, 2 * half))):
        both = sum(dot(left[place, :], right[:, : 2 * units]) for left, right in zip(normed_t, kept))
        down = sum(dot(left[place, :], right[:, 2 * units :]) for left, right in zip(grad_t, kept))
        ref[:, : 2 * units] = both.astype(BF16)
        ref[:, 2 * units :] = down.astype(BF16)


def mlp_grads(normed_t, grad_t, kept, steps, first, count, after=()):
    model = normed_t[0].shape[0]
    rows = sum(array.shape[0] for array in kept)
    target = jax.ShapeDtypeStruct((model // 2, count * kept[0].shape[1] // steps), BF16)
    return kernel_call(
        functools.partial(mlp_grads_kernel, len(kept)),
        "mlp_grads",
        (count,),
        [(array, whole(array)) for array in (*normed_t, *grad_t)]
        + [(array, columns(array, steps, first)) for array in kept],
        [(target.shape, BF16, columns(target, count))] * 2,
        [],
        4 * rows * target.size,
        after,
    )


def attend_back_kernel(group, width, parts, first, last, *refs):
    refs = iter(refs)
    normed, grad, normed_t, grad_t, kept = [[next(refs) for _ in range(parts)] for _ in range(5)]
    weight_ref, cos_ref, sin_ref, gain_q_ref, gain_k_ref, gain_ref, dgain_before_ref = [next(refs) for _ in range(7)]
    before = [] if first else [next(refs) for _ in range(parts)]
    dx = [next(refs) for _ in range(parts)]
    keep_ref, send_ref, dgain_ref, dgain_heads_ref = [next(refs) for _ in range(4)]
    total, dproj = [[next(refs) for _ in range(parts)] for _ in range(2)]
    step = pl.program_id(0)
    wide = group * width
    scaling = float(width**-0.5)
    factor = float(width**-0.5 * np.log2(np.e))
    rot = wide + width
    base = 2 * rot
    out_columns = slice(wide + 2 * width, None)
    in_columns = slice(0, wide + 2 * width)

    @pl.when(step == 0)
    def _():
        for part in range(parts):
            total[part][...] = jnp.zeros_like(total[part]) if first else before[part][...]
        dgain_heads_ref[...] = dgain_before_ref[...]

    half = normed_t[0].shape[0] // 2
    halves = ((keep_ref, slice(0, half)), (send_ref, slice(half, 2 * half)))
    for ref, rows in halves:
        ref[:, out_columns] = sum(
            dot(left[rows, :], right[:, base + width :]) for left, right in zip(grad_t, kept)
        ).astype(BF16)

    def head_back(part, place, head, cotangent):
        gain = gain_q_ref[...] if head < group else gain_k_ref[...]
        raw = kept[part][place, head * width : (head + 1) * width].astype(F32)
        scale = lax.rsqrt(jnp.mean(raw * raw, axis=-1, keepdims=True) + EPSILON)
        unit = raw * scale
        cot = rope_back(cotangent * scaling, cos_ref[...], sin_ref[...])
        row = 0 if head < group else 1
        dgain_heads_ref[row : row + 1, :] += jnp.sum(cot * unit, axis=0, keepdims=True)
        cot = cot * gain
        result = scale * (cot - unit * jnp.mean(unit * cot, axis=-1, keepdims=True))
        dproj[part][place, head * width : (head + 1) * width] = result.astype(BF16)

    for part in range(parts):
        grad_heads = dot(grad[part][...], weight_ref[:, out_columns]).astype(BF16)
        for seq in range(grad_heads.shape[0] // SEQ):
            place = slice(seq * SEQ, (seq + 1) * SEQ)
            keys_rot = kept[part][place, rot + wide : rot + wide + width]
            keys_t = keys_rot.T
            values = kept[part][place, base : base + width]
            dkeys = jnp.zeros((SEQ, width), F32)
            dvalues = jnp.zeros((SEQ, width), F32)
            for head in range(group):
                query_rot = kept[part][place, rot + head * width : rot + (head + 1) * width]
                grad_head = grad_heads[place, head * width : (head + 1) * width]
                exponents = exponents_t(keys_rot, query_rot, factor)
                probs = exponents * (1.0 / jnp.sum(exponents, axis=0, keepdims=True))
                dprobs = dot_t(values, grad_head)
                inner = jnp.sum(probs * dprobs, axis=0, keepdims=True)
                dscores = (probs * (dprobs - inner)).astype(BF16)
                dvalues += dot(probs.astype(BF16), grad_head)
                dkeys += dot(dscores, query_rot)
                head_back(part, place, head, dot(keys_t, dscores).T)
            head_back(part, place, group, dkeys)
            dproj[part][place, wide + width :] = dvalues.astype(BF16)
        total[part][...] += dot_t(dproj[part][...], weight_ref[:, in_columns])

    for ref, rows in halves:
        ref[:, in_columns] = sum(dot(left[rows, :], right[...]) for left, right in zip(normed_t, dproj)).astype(BF16)

    @pl.when(step == pl.num_programs(0) - 1)
    def _():
        for part in range(parts):
            dx[part][...] = total[part][...].astype(dx[part].dtype)
        if last:
            dgain_ref[...] = (
                sum(
                    jnp.sum(left[...].astype(F32) * right[...], axis=0, keepdims=True)
                    for left, right in zip(normed, total)
                )
                / gain_ref[...]
            )
        else:
            dgain_ref[...] = jnp.zeros_like(dgain_ref)


def attend_back(
    normed, grad, normed_t, grad_t, kept, weights, tables, gains, heads, group, width, first, count, before, after=()
):
    model = weights.shape[0]
    last = first + count == heads
    dx_before, dgain_before = before
    half = jax.ShapeDtypeStruct((model // 2, count * weights.shape[1] // heads), BF16)
    rows = sum(array.shape[0] for array in normed)
    block = weights.shape[1] // heads
    results = kernel_call(
        functools.partial(attend_back_kernel, group, width, len(normed), not dx_before, last),
        "attend_back",
        (count,),
        [(array, whole(array)) for array in (*normed, *grad, *normed_t, *grad_t)]
        + [(array, columns(array, heads, first)) for array in (*kept, weights)]
        + [(array, whole(array)) for array in (*tables, *gains, dgain_before, *dx_before)],
        [(array.shape, BF16 if last else F32, whole(array)) for array in normed]
        + [(half.shape, BF16, columns(half, count))] * 2
        + [(gains[-1].shape, F32, whole(gains[-1])), (dgain_before.shape, F32, whole(dgain_before))],
        [pltpu.VMEM(array.shape, F32) for array in normed]
        + [pltpu.VMEM((array.shape[0], (group + 2) * width), BF16) for array in normed],
        count * (4 * rows * model * block + 10 * rows * SEQ * group * width),
        after,
    )
    parts = len(normed)
    return results[:parts], *results[parts:]


def unit_rows(values):
    scale = lax.rsqrt(jnp.mean(values * values, axis=-1, keepdims=True) + EPSILON)
    return values * scale, scale


def norm_back(unit, scale, cotangent):
    return scale * (cotangent - unit * jnp.mean(unit * cotangent, axis=-1, keepdims=True))


def pack(parts, pieces):
    rows = parts[0].shape[0]
    split = [part.reshape(rows, pieces, part.shape[1] // pieces) for part in parts]
    return jnp.concatenate(split, axis=2).reshape(rows, -1)


def unpack(packed, pieces, widths):
    rows = packed.shape[0]
    split = packed.reshape(rows, pieces, -1).astype(F32)
    ends = np.cumsum([width // pieces for width in widths])
    return [
        split[:, :, end - width // pieces : end].reshape(rows, width) for end, width in zip(ends, widths)
    ]


def relative_places(size):
    relative = jnp.arange(size, dtype=jnp.int32) ^ lax.axis_index("dp")
    layers = size // 4
    return (relative & 1) * (2 * layers) + ((relative >> 1) & 1) * layers + (relative >> 2)


def exchange(array, axis, size, flip):
    return lax.ppermute(array, axis, [(index, index ^ flip) for index in range(size)])


def add(terms):
    total = terms[0].astype(F32)
    for term in terms[1:]:
        total = total + term.astype(F32)
    return total


class BlockSum:
    def __init__(self, size, keep, send):
        self.size = size
        layers = size // 4
        self.flips = [2] + [4 << bit for bit in reversed(range(layers.bit_length() - 1))]
        got = exchange(send, "dp", size, 1)
        shape = (2,) * len(self.flips) + (-1, keep.shape[1])
        self.terms = [keep.reshape(shape), got.reshape(shape)]

    def halve(self, flip):
        axis = self.flips.index(flip)
        self.flips.pop(axis)
        sent = add([lax.index_in_dim(term, 1, axis, keepdims=False) for term in self.terms]).astype(BF16)
        self.terms = [lax.index_in_dim(term, 0, axis, keepdims=False) for term in self.terms]
        self.terms.append(exchange(sent, "dp", self.size, flip))
        return sent

    def finish(self):
        while self.flips:
            self.halve(self.flips[-1])
        return add(self.terms)


def body(
    dp_size,
    tensor_size,
    inputs,
    grad_out,
    w_query,
    key_weight,
    value_weight,
    w_output,
    w_gate,
    w_up,
    w_down,
    gain_attn,
    gain_mlp,
    gain_query,
    gain_keys,
):
    own_rows, model = inputs.shape
    width = gain_query.shape[0]
    heads = key_weight.shape[1] // width
    group = w_query.shape[1] // key_weight.shape[1]
    hidden = w_gate.shape[1]
    steps = max(1, hidden // 256)
    by_pair = tensor_size == 2 and own_rows % SEQ == 0

    def gather_rows(own):
        if by_pair:
            return [own, exchange(own, "tensor", 2, 1)]
        return [lax.all_gather(own, "tensor", axis=0, tiled=True)]

    def sum_rows(parts):
        if by_pair:
            return add([parts[0], exchange(parts[1], "tensor", 2, 1)])
        return lax.psum_scatter(parts[0], "tensor", scatter_dimension=0, tiled=True).astype(F32)

    tables = rope_tables(width)
    gains = gain_query[None, :], gain_keys[None, :], gain_attn[None, :]
    places = relative_places(dp_size)
    attn_weights = lax.all_gather(
        pack([w_query, key_weight, value_weight, w_output.T], heads), "dp", axis=0, tiled=True
    )
    mlp_weights = lax.all_gather(pack([w_gate, w_up, w_down.T], steps), "dp", axis=0, tiled=True)

    inputs_f = inputs.astype(F32)
    unit_in, scale_in = unit_rows(inputs_f)
    normed = gather_rows((unit_in * gain_attn).astype(BF16))
    grad_rows = gather_rows(grad_out)
    normed_t = [turn(places, array) for array in normed]
    grad_t = [turn(places, array) for array in grad_rows]

    parts, kept = [], []
    after = [*normed_t, *grad_t]
    for array in reversed(normed):
        part, held = attend(array, attn_weights, tables, *gains[:2], heads, group, width, after)
        parts.insert(0, part)
        kept.insert(0, held)
        after = [part]
    middle = inputs_f + sum_rows(parts)
    unit_mid, scale_mid = unit_rows(middle)
    normed_mlp = gather_rows((unit_mid * gain_mlp).astype(BF16))

    ffn_parts, dx_parts, kept_mlp, dgain_mlp, after = [], [], [], 0.0, []
    for array, grad in zip(normed_mlp, grad_rows):
        ffn, dx, held, dgain = mlp(array, grad, mlp_weights, gain_mlp[None, :], steps, after)
        ffn_parts.append(ffn)
        dx_parts.append(dx)
        kept_mlp.append(held)
        dgain_mlp = dgain_mlp + dgain[0]
        after = [dx]
    normed_mlp_t = [turn(places, array, after) for array in normed_mlp]
    grad_normed_mlp = sum_rows(dx_parts)
    grad_middle = grad_out.astype(F32) + norm_back(unit_mid, scale_mid, grad_normed_mlp * gain_mlp)
    grad_attended = gather_rows(grad_middle.astype(BF16))
    grad_attended_t = [turn(places, array) for array in grad_attended]

    first = max(1, steps // 2)
    mlp_sums, after = [], []
    for cut in [(0, first), (first, steps - first)] if steps > 1 else [(0, 1)]:
        keep, send = mlp_grads(normed_mlp_t, grad_t, kept_mlp, steps, *cut, after)
        mlp_sums.append(BlockSum(dp_size, keep, send))
        after = [keep]
    x_flip, z_flip = 2, 4
    after = [block_sum.halve(flip) for block_sum, flip in zip(mlp_sums, (x_flip, z_flip))]

    first = max(1, heads // 2)
    before = ((), jnp.zeros((8, width), F32))
    attn_sums = []
    for cut in [(0, first), (first, heads - first)] if heads > 1 else [(0, 1)]:
        dx_parts, keep, send, dgain_attn, dgain_heads = attend_back(
            normed, grad_attended, normed_t, grad_attended_t, kept, attn_weights, tables, gains,
            heads, group, width, *cut, before, after,
        )
        before = (dx_parts, dgain_heads)
        if not attn_sums:
            after = [block_sum.halve(flip) for block_sum, flip in zip(mlp_sums, (z_flip, x_flip))]
        attn_sums.append(BlockSum(dp_size, keep, send))
        after = [*after, attn_sums[-1].halve(x_flip)]

    sums = jnp.concatenate([dgain_attn[0], dgain_mlp, dgain_heads[0], dgain_heads[1]]).reshape(-1, 128)
    for axis, size in (("dp", dp_size), ("tensor", tensor_size)):
        for bit in range(size.bit_length() - 1):
            sums = sums + exchange(sums, axis, size, 1 << bit)
    sums = sums.reshape(-1)

    grad_normed = sum_rows(dx_parts)
    grad_inputs = (grad_middle + norm_back(unit_in, scale_in, grad_normed * gain_attn)).astype(BF16)
    layer_out = (middle + sum_rows(ffn_parts)).astype(BF16)
    mlp_parts = jnp.concatenate([block_sum.finish() for block_sum in mlp_sums], axis=1)
    attn_parts = jnp.concatenate([block_sum.finish() for block_sum in attn_sums], axis=1)
    query_part, keys_part, values_part, output_part = unpack(
        attn_parts, heads, [w_query.shape[1], key_weight.shape[1], value_weight.shape[1], w_output.shape[0]]
    )
    gate_part, up_part, down_part = unpack(mlp_parts, steps, [hidden, hidden, hidden])
    return (
        layer_out,
        grad_inputs,
        query_part,
        keys_part,
        values_part,
        output_part.T,
        gate_part,
        up_part,
        down_part.T,
        sums[:model],
        sums[model : 2 * model],
        sums[2 * model : 2 * model + width],
        sums[2 * model + width :],
    )


def solution(mesh):
    rows = P(("dp", "tensor"), None)
    wide, tall = P("dp", "tensor"), P("tensor", "dp")
    return jax.shard_map(
        functools.partial(body, mesh.shape["dp"], mesh.shape["tensor"]),
        mesh=mesh,
        in_specs=(rows, rows, wide, wide, wide, tall, wide, wide, tall, P(), P(), P(), P()),
        out_specs=(rows, rows, wide, wide, wide, tall, wide, wide, tall, P(), P(), P(), P()),
        check_vma=False,
    )
```

```python
import functools

import jax
import jax.numpy as jnp
import numpy as np
from jax import lax
from jax.experimental import pallas as pl
from jax.experimental.pallas import tpu as pltpu
from jax.sharding import PartitionSpec as P

SEQ = 512
EPSILON = 1e-06
THETA = 1000000.0
F32 = jnp.float32
BF16 = jnp.bfloat16
VMEM_LIMIT = 56 * 1024 * 1024
QUERY_TILE = 256
KEY_TILE = 128


def dot(left, right):
    return lax.dot_general(left, right, (((1,), (0,)), ((), ())), preferred_element_type=F32)


def dot_t(left, right):
    return lax.dot_general(left, right, (((1,), (1,)), ((), ())), preferred_element_type=F32)


def whole(array):
    dims = array.shape
    return pl.BlockSpec(dims, lambda *_: (0,) * len(dims))


def columns(array, count, first=0):
    return pl.BlockSpec((array.shape[0], array.shape[1] // count), lambda j: (0, first + j))


def kernel_call(kernel, name, grid, inputs, outputs, scratch, flops, after=(), into=(), into_index=0):
    after = [*into, *after]
    known = len(inputs)

    def run(*refs):
        kernel(*refs[:known], *refs[known + len(after) :])

    moved = sum(array.size * array.dtype.itemsize for array, _ in inputs)
    return pl.pallas_call(
        run,
        grid=grid,
        in_specs=[spec for _, spec in inputs] + [pl.BlockSpec(memory_space=pl.ANY)] * len(after),
        out_specs=[spec for _, _, spec in outputs],
        out_shape=[jax.ShapeDtypeStruct(shape, dtype) for shape, dtype, _ in outputs],
        scratch_shapes=scratch,
        input_output_aliases={known + index: into_index + index for index in range(len(into))},
        compiler_params=pltpu.CompilerParams(vmem_limit_bytes=VMEM_LIMIT),
        cost_estimate=pl.CostEstimate(flops=64 * flops, bytes_accessed=64 * moved if flops else 1, transcendentals=0),
        name=name,
    )(*[array for array, _ in inputs], *after)


def sync(*arrays):
    spec = pl.BlockSpec(memory_space=pl.ANY)
    return kernel_call(
        lambda *_: None, "sync", (), [], [(array.shape, array.dtype, spec) for array in arrays], [], 0, (), arrays
    )


def rope_tables(width):
    half = width // 2
    places = np.arange(SEQ, dtype=np.float32)
    inverse = (THETA ** (-2.0 * np.arange(half, dtype=np.float32) / width)).astype(np.float32)
    angles = places[:, None] * inverse[None, :]
    cosine = np.concatenate([np.cos(angles), np.cos(angles)], axis=-1)
    sine = np.concatenate([-np.sin(angles), np.sin(angles)], axis=-1)
    return cosine.astype(np.float32), sine.astype(np.float32)


def rope(values, cosine, sine):
    half = values.shape[-1] // 2
    return values * cosine + pltpu.roll(values, half, 1) * sine


def rope_back(values, cosine, sine):
    half = values.shape[-1] // 2
    return values * cosine + pltpu.roll(values * sine, half, 1)


def score_tiles():
    for query in range(0, SEQ, QUERY_TILE):
        for key in range(0, query + QUERY_TILE, KEY_TILE):
            yield slice(key, key + KEY_TILE), slice(query, query + QUERY_TILE)


def exponents_t(keys_rot, query_rot, factor, keys, queries):
    result = jnp.exp2(dot_t(keys_rot, query_rot) * factor)
    if keys.stop - 1 <= queries.start:
        return result
    key_place = lax.broadcasted_iota(jnp.int32, result.shape, 0) + keys.start
    query_place = lax.broadcasted_iota(jnp.int32, result.shape, 1) + queries.start
    return jnp.where(key_place <= query_place, result, 0.0)


def load_weights(cuts, chunks, weight_ref):
    step = pl.program_id(0)
    for index, (first, count) in enumerate(cuts):
        places_ref, *halves = chunks[3 * index : 3 * index + 3]

        @pl.when((step >= first) & (step < first + count))
        def _():
            blocks = places_ref.shape[0]
            block = weight_ref.shape[0] // blocks
            for position in range(blocks):
                half, inner = halves[2 * position // blocks], position % (blocks // 2)
                place = pl.ds(pl.multiple_of(places_ref[position] * block, block), block)
                weight_ref[place, :] = half[inner * block : (inner + 1) * block, :]


def weight_inputs(cuts, chunks):
    inputs = []
    for (first, count), (places, *halves) in zip(cuts, chunks):
        inputs.append((places, pl.BlockSpec(memory_space=pltpu.SMEM)))
        for half in halves:
            spec = pl.BlockSpec(
                (half.shape[0], half.shape[1] // count),
                lambda j, first=first, count=count: (0, jnp.clip(j - first, 0, count - 1)),
            )
            inputs.append((half, spec))
    return inputs


def attend_kernel(group, width, cuts, normed_ref, cos_ref, sin_ref, gain_q_ref, gain_k_ref, *refs):
    chunks, (part_ref, sums_ref, kept_ref, out_ref, total, weight_ref) = refs[: 3 * len(cuts)], refs[3 * len(cuts) :]
    step = pl.program_id(0)
    load_weights(cuts, chunks, weight_ref)
    rows = normed_ref.shape[0]
    wide = group * width
    factor = float(width**-0.5 * np.log2(np.e))
    proj = dot(normed_ref[...], weight_ref[:, : wide + 2 * width])
    kept_ref[:, : wide + width] = proj[:, : wide + width].astype(BF16)
    values = proj[:, wide + width :].astype(BF16)
    kept_ref[:, 2 * (wide + width) :] = values
    for seq in range(rows // SEQ):
        place = slice(seq * SEQ, (seq + 1) * SEQ)
        rotated = []
        for head in range(group + 1):
            raw = proj[place, head * width : (head + 1) * width]
            scale = lax.rsqrt(jnp.mean(raw * raw, axis=-1, keepdims=True) + EPSILON)
            gain = gain_q_ref[...] if head < group else gain_k_ref[...]
            turned = rope(raw * scale * gain, cos_ref[...], sin_ref[...]).astype(BF16)
            kept_ref[place, wide + width + head * width : wide + width + (head + 1) * width] = turned
            rotated.append(turned)
        values_t = values[place].T
        for head in range(group):
            out_t, sums = {}, {}
            for keys, queries in score_tiles():
                exponents = exponents_t(rotated[group][keys], rotated[head][queries], factor, keys, queries)
                start = queries.start
                sums[start] = sums.get(start, 0.0) + jnp.sum(exponents, axis=0, keepdims=True)
                out_t[start] = out_t.get(start, 0.0) + dot(values_t[:, keys], exponents.astype(BF16))
            for start in out_t:
                scale = 1.0 / sums[start]
                spot = slice(seq * SEQ + start, seq * SEQ + start + QUERY_TILE)
                sums_ref[head : head + 1, spot] = scale
                out_ref[spot, head * width : (head + 1) * width] = (out_t[start] * scale).T.astype(BF16)
    out = dot_t(out_ref[...], weight_ref[:, wide + 2 * width :])

    @pl.when(step == 0)
    def _():
        total[...] = out

    @pl.when(step > 0)
    def _():
        total[...] += out

    @pl.when(step == pl.num_programs(0) - 1)
    def _():
        part_ref[...] = total[...].astype(BF16)


def part_rows(rows, width, steps, part, parts):
    return (parts * rows, width), BF16, pl.BlockSpec((rows, width // steps), lambda j: (part, j))


def attend(normed, cuts, chunks, tables, gain_q, gain_k, group, width, part, parts, after=(), into=()):
    rows, model = normed.shape
    heads = sum(count for _, count in cuts)
    block = (2 * group + 2) * width
    return kernel_call(
        functools.partial(attend_kernel, group, width, cuts),
        "attend",
        (heads,),
        [(array, whole(array)) for array in (normed, *tables, gain_q, gain_k)] + weight_inputs(cuts, chunks),
        [
            (normed.shape, BF16, whole(normed)),
            ((8 * heads, rows), F32, pl.BlockSpec((8, rows), lambda j: (j, 0))),
            part_rows(rows, heads * (2 * group + 3) * width, heads, part, parts),
            part_rows(rows, heads * group * width, heads, part, parts),
        ],
        [pltpu.VMEM((rows, model), F32), pltpu.VMEM((model, block), BF16)],
        heads * (2 * rows * model * block + 4 * rows * SEQ * group * width),
        after,
        into,
        2,
    )


def turn_kernel(places_ref, *refs):
    target_ref = refs[-1]
    count = places_ref.shape[0]
    block = target_ref.shape[0] // count
    for index in range(count):
        place = pl.ds(pl.multiple_of(places_ref[index] * block, block), block)
        begin = 0
        for source_ref in refs[:-1]:
            rows = source_ref.shape[0]
            target_ref[place, begin : begin + rows] = source_ref[:, index * block : (index + 1) * block].T
            begin += rows


def turn(places, sources, part, parts, after=(), into=(), flops=0):
    rows, model = sources[0].shape
    width = rows * len(sources)
    return kernel_call(
        turn_kernel,
        "turn",
        (1,),
        [(places, pl.BlockSpec(memory_space=pltpu.SMEM))] + [(source, whole(source)) for source in sources],
        [((model, rows * parts), BF16, pl.BlockSpec((model, width), lambda j: (0, part // len(sources))))],
        [],
        flops,
        after,
        into,
    )


def mlp_kernel(cuts, normed_ref, grad_ref, gain_ref, *refs):
    chunks = refs[: 3 * len(cuts)]
    out_ref, dx_ref, dgain_ref, both_ref, hidden_ref, out_total, dx_total, weight_ref = refs[3 * len(cuts) :]
    step = pl.program_id(0)
    units = weight_ref.shape[1] // 3
    load_weights(cuts, chunks, weight_ref)

    @pl.when(step == 0)
    def _():
        out_total[...] = jnp.zeros_like(out_total)
        dx_total[...] = jnp.zeros_like(dx_total)

    both = dot(normed_ref[...], weight_ref[:, : 2 * units])
    gate, up = both[:, :units], both[:, units:]
    sig = 1.0 / (1.0 + jnp.exp(-gate))
    silu = gate * sig
    hidden = (silu * up).astype(BF16)
    grad_hidden = dot(grad_ref[...], weight_ref[:, 2 * units :])
    both_ref[:, :units] = (grad_hidden * up * (sig + silu * (1.0 - sig))).astype(BF16)
    both_ref[:, units:] = (grad_hidden * silu).astype(BF16)
    hidden_ref[...] = hidden
    out_total[...] += dot_t(hidden, weight_ref[:, 2 * units :])
    dx_total[...] += dot_t(both_ref[...], weight_ref[:, : 2 * units])

    @pl.when(step == pl.num_programs(0) - 1)
    def _():
        out_ref[...] = out_total[...].astype(BF16)
        dx_ref[...] = dx_total[...].astype(BF16)
        dgain_ref[...] = (
            jnp.sum(normed_ref[...].astype(F32) * dx_total[...], axis=0, keepdims=True) / gain_ref[...]
        )


def mlp(normed, grad_rows, gain, cuts, chunks, part, parts, after=(), into=()):
    rows, model = normed.shape
    steps = sum(count for _, count in cuts)
    units = chunks[0][1].shape[1] // cuts[0][1] // 3
    return kernel_call(
        functools.partial(mlp_kernel, cuts),
        "mlp",
        (steps,),
        [(array, whole(array)) for array in (normed, grad_rows, gain)] + weight_inputs(cuts, chunks),
        [
            (normed.shape, BF16, whole(normed)),
            (normed.shape, BF16, whole(normed)),
            (gain.shape, F32, whole(gain)),
            part_rows(rows, steps * 2 * units, steps, part, parts),
            part_rows(rows, steps * units, steps, part, parts),
        ],
        [pltpu.VMEM((rows, model), F32), pltpu.VMEM((rows, model), F32), pltpu.VMEM((model, 3 * units), BF16)],
        12 * rows * model * steps * units,
        after,
        into,
        3,
    )


def weight_grads_kernel(in_t, out_t, into, outof, *halves):
    wide = into.shape[1]
    half = in_t.shape[0] // 2
    *halves, token_ref = halves
    token_ref[...] = jnp.zeros_like(token_ref)
    for ref, place in zip(halves, (slice(0, half), slice(half, 2 * half))):
        ref[:, :wide] = dot(in_t[place, :], into[...]).astype(BF16)
        ref[:, wide:] = dot(out_t[place, :], outof[...]).astype(BF16)


def weight_grads(in_t, out_t, into, outof, steps, first, count, after=(), hides=True):
    model, rows = in_t.shape
    token = jax.ShapeDtypeStruct((8, 128), F32)
    target = jax.ShapeDtypeStruct((model // 2, count * (into.shape[1] + outof.shape[1]) // steps), BF16)
    return kernel_call(
        weight_grads_kernel,
        "weight_grads",
        (count,),
        [(in_t, whole(in_t)), (out_t, whole(out_t))]
        + [(array, columns(array, steps, first)) for array in (into, outof)],
        [(target.shape, BF16, columns(target, count))] * 2 + [(token.shape, F32, whole(token))],
        [],
        4 * rows * target.size if hides else 0,
        after,
    )


def attend_back_kernel(
    group, width, cuts, grad_ref, kept, out_ref, sums_ref, cos_ref, sin_ref, gain_q_ref, gain_k_ref, *refs
):
    chunks = refs[: 3 * len(cuts)]
    dx_ref, dgain_ref, dproj, total, weight_ref = refs[3 * len(cuts) :]
    step = pl.program_id(0)
    load_weights(cuts, chunks, weight_ref)
    wide = group * width
    scaling = float(width**-0.5)
    factor = float(width**-0.5 * np.log2(np.e))
    rot = wide + width
    base = 2 * rot

    @pl.when(step == 0)
    def _():
        total[...] = jnp.zeros_like(total)
        dgain_ref[...] = jnp.zeros_like(dgain_ref)

    def head_back(place, head, cotangent):
        gain = gain_q_ref[...] if head < group else gain_k_ref[...]
        raw = kept[place, head * width : (head + 1) * width].astype(F32)
        scale = lax.rsqrt(jnp.mean(raw * raw, axis=-1, keepdims=True) + EPSILON)
        unit = raw * scale
        cot = rope_back(cotangent * scaling, cos_ref[...], sin_ref[...])
        row = 0 if head < group else 1
        dgain_ref[row : row + 1, :] += jnp.sum(cot * unit, axis=0, keepdims=True)
        cot = cot * gain
        result = scale * (cot - unit * jnp.mean(unit * cot, axis=-1, keepdims=True))
        dproj[place, head * width : (head + 1) * width] = result.astype(BF16)

    grad_heads = dot(grad_ref[...], weight_ref[:, wide + 2 * width :]).astype(BF16)
    for seq in range(grad_heads.shape[0] // SEQ):
        place = slice(seq * SEQ, (seq + 1) * SEQ)
        keys_rot = kept[place, rot + wide : rot + wide + width]
        keys_t = keys_rot.T
        values = kept[place, base : base + width]
        dkeys, dvalues = [{key: 0.0 for key in range(0, SEQ, KEY_TILE)} for _ in range(2)]
        for head in range(group):
            query_rot = kept[place, rot + head * width : rot + (head + 1) * width]
            grad_head = grad_heads[place, head * width : (head + 1) * width]
            weighted = grad_head.astype(F32) * out_ref[place, head * width : (head + 1) * width].astype(F32)
            inner = jnp.sum(weighted.T, axis=0, keepdims=True)
            scale = sums_ref[head : head + 1, place]
            dqueries = {}
            for keys, queries in score_tiles():
                exponents = exponents_t(keys_rot[keys], query_rot[queries], factor, keys, queries)
                probs = exponents * scale[:, queries]
                dprobs = dot_t(values[keys], grad_head[queries])
                dscores = (probs * (dprobs - inner[:, queries])).astype(BF16)
                dvalues[keys.start] += dot(probs.astype(BF16), grad_head[queries])
                dkeys[keys.start] += dot(dscores, query_rot[queries])
                start = queries.start
                dqueries[start] = dqueries.get(start, 0.0) + dot(keys_t[:, keys], dscores)
            head_back(place, head, jnp.concatenate([dqueries[start].T for start in dqueries], axis=0))
        dkeys = jnp.concatenate(list(dkeys.values()), axis=0)
        dvalues = jnp.concatenate(list(dvalues.values()), axis=0)
        head_back(place, group, dkeys)
        dproj[place, wide + width :] = dvalues.astype(BF16)
    total[...] += dot_t(dproj[...], weight_ref[:, : wide + 2 * width])

    @pl.when(step == pl.num_programs(0) - 1)
    def _():
        dx_ref[...] = total[...].astype(BF16)


def attend_back(grad, kept, head_out, sums, cuts, chunks, tables, gain_q, gain_k, group, width, part, parts, after=(), into=()):
    rows, model = grad.shape
    heads = sum(count for _, count in cuts)
    block = (2 * group + 2) * width
    return kernel_call(
        functools.partial(attend_back_kernel, group, width, cuts),
        "attend_back",
        (heads,),
        [
            (grad, whole(grad)),
            (kept, pl.BlockSpec((rows, kept.shape[1] // heads), lambda j: (part, j))),
            (head_out, pl.BlockSpec((rows, head_out.shape[1] // heads), lambda j: (part, j))),
            (sums, pl.BlockSpec((8, rows), lambda j: (j, 0))),
            *[(array, whole(array)) for array in (*tables, gain_q, gain_k)],
            *weight_inputs(cuts, chunks),
        ],
        [
            (grad.shape, BF16, whole(grad)),
            ((8, width), F32, pl.BlockSpec((8, width), lambda j: (0, 0))),
            part_rows(rows, heads * (group + 2) * width, heads, part, parts),
        ],
        [pltpu.VMEM((rows, model), F32), pltpu.VMEM((model, block), BF16)],
        heads * (2 * rows * model * block + 10 * rows * SEQ * group * width),
        after,
        into,
        2,
    )


def unit_rows(values):
    scale = lax.rsqrt(jnp.mean(values * values, axis=-1, keepdims=True) + EPSILON)
    return values * scale, scale


def norm_back(unit, scale, cotangent):
    return scale * (cotangent - unit * jnp.mean(unit * cotangent, axis=-1, keepdims=True))


def pack(parts, pieces):
    rows = parts[0].shape[0]
    split = [part.reshape(rows, pieces, part.shape[1] // pieces) for part in parts]
    return jnp.concatenate(split, axis=2).reshape(rows, -1)


def unpack(packed, pieces, widths):
    rows = packed.shape[0]
    split = packed.reshape(rows, pieces, -1).astype(F32)
    ends = np.cumsum([width // pieces for width in widths])
    return [
        split[:, :, end - width // pieces : end].reshape(rows, width) for end, width in zip(ends, widths)
    ]


def relative_places(size):
    relative = jnp.arange(size, dtype=jnp.int32) ^ lax.axis_index("dp")
    layers = size // 4
    return (relative & 1) * (2 * layers) + ((relative >> 1) & 1) * layers + (relative >> 2)


def exchange(array, axis, size, flip):
    return lax.ppermute(array, axis, [(index, index ^ flip) for index in range(size)])


def z_bits(size):
    return [4 << bit for bit in reversed(range((size // 4).bit_length() - 1))]


class BlockGather:
    def __init__(self, size, block, flips):
        self.size, self.flips = size, list(flips)
        self.held, self.done, self.got = block, 0, None

    def start(self):
        self.got = exchange(self.held, "dp", self.size, self.flips[self.done])
        self.done += 1

    def join(self):
        self.held = jnp.concatenate([self.held, self.got], axis=0)

    def chunk(self):
        position = jnp.arange(self.size, dtype=jnp.int32)
        place = lax.axis_index("dp") ^ sum(
            ((position >> bit) & 1) * flip for bit, flip in enumerate(self.flips)
        )
        return place, self.held, self.got


class BlockSum:
    def __init__(self, size, keep, send, flips):
        self.size, self.flips = size, list(flips)
        self.bits = [2, *z_bits(size)]
        self.left = list(self.bits)
        self.shape = (2,) * len(self.bits) + (-1, keep.shape[1])
        self.terms = [(keep.reshape(self.shape), self.bits)]
        self.got = exchange(send, "dp", size, 1)

    def part(self, flip=None):
        total = 0.0
        for array, bits in self.terms:
            start = [int(bit == flip) for bit in bits] + [0, 0]
            stop = [
                int(bit == flip) + 1 if bit == flip or bit not in self.left else 2 for bit in bits
            ] + list(array.shape[-2:])
            piece = lax.slice(array, start, stop)
            total = total + piece.reshape((2,) * (len(self.left) - (flip is not None)) + piece.shape[-2:]).astype(F32)
        return total

    def take(self):
        if len(self.terms) == 1:
            self.got = self.got.reshape(self.shape)
        self.terms.append((self.got, list(self.left)))

    def halve(self):
        self.take()
        flip = self.flips.pop(0)
        sent = self.part(flip).astype(BF16)
        self.left.remove(flip)
        self.got = exchange(sent, "dp", self.size, flip)
        return sent

    def finish(self):
        self.take()
        return self.part()


def arrive(movers, *others):
    results = sync(*[mover.got for mover in movers], *others)
    for mover, got in zip(movers, results):
        mover.got = got
    return results[len(movers) :]


def body(
    dp_size,
    tensor_size,
    inputs,
    grad_out,
    w_query,
    key_weight,
    value_weight,
    w_output,
    w_gate,
    w_up,
    w_down,
    gain_attn,
    gain_mlp,
    gain_query,
    gain_keys,
):
    own_rows, model = inputs.shape
    width = gain_query.shape[0]
    heads = key_weight.shape[1] // width
    group = w_query.shape[1] // key_weight.shape[1]
    hidden = w_gate.shape[1]
    steps = max(1, hidden // 256)
    by_pair = tensor_size == 2 and own_rows % SEQ == 0
    part_count = 2 if by_pair else 1

    def start_rows(own):
        if by_pair:
            return exchange(own, "tensor", 2, 1)
        return lax.all_gather(own, "tensor", axis=0, tiled=True)

    def all_rows(own, got):
        return [own, got] if by_pair else [got]

    def start_sum(parts):
        if by_pair:
            return exchange(parts[1], "tensor", 2, 1)
        return lax.psum_scatter(parts[0], "tensor", scatter_dimension=0, tiled=True)

    def add_sum(parts, got, base=0.0):
        total = base + got.astype(F32)
        return total + parts[0].astype(F32) if by_pair else total

    tables = rope_tables(width)
    gains = gain_query[None, :], gain_keys[None, :]
    places = relative_places(dp_size)
    z_flips = z_bits(dp_size)
    x_flip, z_flip, z_first = 2, z_flips[-1], z_flips[:-1]

    def gather_start(packed, steps):
        first = max(1, steps // 2)
        cuts = [(0, first), (first, steps - first)] if steps > 1 else [(0, 1)]
        unit = packed.shape[1] // steps
        orders = [*z_first, z_flip, x_flip, 1], [*z_first, x_flip, z_flip, 1]
        return cuts, [
            BlockGather(dp_size, packed[:, start * unit : (start + count) * unit], flips)
            for (start, count), flips in zip(cuts, orders)
        ]

    attn_cuts, attn_gathers = gather_start(pack([w_query, key_weight, value_weight, w_output.T], heads), heads)
    inputs_f = inputs.astype(F32)
    unit_in, scale_in = unit_rows(inputs_f)
    normed_own = (unit_in * gain_attn).astype(BF16)
    for gather in attn_gathers:
        gather.start()
    grad_t = turn(places, [grad_out], 0, part_count) if by_pair else ()
    normed_t = turn(places, [normed_own], 0, part_count) if by_pair else ()
    half = own_rows // 2
    grad_half = start_rows(grad_out[:half]) if by_pair else start_rows(grad_out)
    grad_half, packed, *turned = arrive(
        attn_gathers, grad_half, pack([w_gate, w_up, w_down.T], steps), *grad_t, *normed_t
    )
    grad_t, normed_t = turned[:1], turned[1:]

    mlp_cuts, mlp_gathers = gather_start(packed, steps)
    while attn_gathers[0].done < len(attn_gathers[0].flips) - 2:
        for gather in attn_gathers:
            gather.join()
            gather.start()
        arrive(attn_gathers)
    for gather in attn_gathers:
        gather.join()
        gather.start()
    for gather in mlp_gathers:
        gather.start()
    normed_got = start_rows(normed_own)
    (normed_got,) = arrive([*attn_gathers, *mlp_gathers], normed_got)
    normed = all_rows(normed_own, normed_got)
    for gather in attn_gathers:
        gather.join()
        gather.start()
    arrive(attn_gathers)
    attn_chunks = [gather.chunk() for gather in attn_gathers]

    def grow_mlp():
        sent = []
        if mlp_gathers[0].done < len(mlp_gathers[0].flips):
            for gather in mlp_gathers:
                gather.join()
                gather.start()
                sent.append(gather.held)
        return sent

    parts, row_sums, kept = [None] * part_count, [None] * part_count, ()
    grad_rest = start_rows(grad_out[half:]) if by_pair else None
    for index in reversed(range(part_count)):
        after = grow_mlp()
        parts[index], row_sums[index], *kept = attend(
            normed[index], attn_cuts, attn_chunks, tables, *gains, group, width, index, part_count, after, kept
        )
        if index == part_count - 1:
            if by_pair:
                parts[index], grad_rest = arrive(mlp_gathers, parts[index], grad_rest)
            else:
                (parts[index],) = arrive(mlp_gathers, parts[index])
            part_got = start_sum(parts)
    parts[0], part_got = arrive(mlp_gathers, parts[0], part_got)
    kept, head_out = kept
    while mlp_gathers[0].done < len(mlp_gathers[0].flips):
        grow_mlp()
        arrive(mlp_gathers)
    mlp_chunks = [gather.chunk() for gather in mlp_gathers]
    grad_rows = [grad_out, jnp.concatenate([grad_half, grad_rest], axis=0)] if by_pair else [grad_half]
    middle = add_sum(parts, part_got, inputs_f)
    unit_mid, scale_mid = unit_rows(middle)
    normed_own = (unit_mid * gain_mlp).astype(BF16)
    normed_got = start_rows(normed_own)

    def run_mlp(index, array, after, into):
        return mlp(
            array, grad_rows[index], gain_mlp[None, :], mlp_cuts, mlp_chunks, index, part_count, after, into
        )

    if by_pair:
        ffn, dx, dgain, *kept_mlp = run_mlp(0, normed_own, [normed_own], ())
        grad_t = turn(places, grad_rows[1:], 1, part_count, [dx], grad_t)
        normed_t = turn(places, normed[1:], 1, part_count, grad_t, normed_t)
        dx, normed_got, *turned = sync(dx, normed_got, *grad_t, *normed_t)
        grad_t, normed_t = turned[:1], turned[1:]
        ffn_parts, dx_parts, dgain_mlp = [ffn], [dx], dgain[0]
        ffn, dx, dgain, *kept_mlp = run_mlp(1, normed_got, [dx], kept_mlp)
        ffn_parts.append(ffn)
        dx_parts.append(dx)
        dgain_mlp = dgain_mlp + dgain[0]
        after = [dx]
    else:
        grad_t = turn(places, grad_rows, 0, 1)
        normed_t = turn(places, normed, 0, 1)
        ffn, dx, dgain, *kept_mlp = run_mlp(0, normed_got, (), ())
        ffn_parts, dx_parts, dgain_mlp = [ffn], [dx], dgain[0]
        after = [dx]
    normed_mlp_t = turn(places, all_rows(normed_own, normed_got), 0, part_count, after, flops=10**9)

    dx_got = start_sum(dx_parts)
    orders = [x_flip, z_flip, *z_first], [z_flip, x_flip, *z_first]

    def mlp_weight_grads(index, after):
        keep, send, token = weight_grads(
            *normed_mlp_t, *grad_t, *kept_mlp, steps, *mlp_cuts[index], after, index > 0
        )
        return token, BlockSum(dp_size, keep, send, orders[index])

    keep, block_sum = mlp_weight_grads(0, after)
    mlp_sums = [block_sum]
    keep, dx_got = sync(keep, dx_got)
    grad_middle = grad_out.astype(F32) + norm_back(unit_mid, scale_mid, add_sum(dx_parts, dx_got) * gain_mlp)
    attended_own = grad_middle.astype(BF16)
    attended_got = start_rows(attended_own)
    after = [attended_own]
    if len(mlp_cuts) > 1:
        keep, block_sum = mlp_weight_grads(1, after)
        mlp_sums.append(block_sum)
        after = [keep]
    attended_t = turn(places, [attended_own], 0, part_count, after) if by_pair else ()
    keep, *attended_t = arrive(mlp_sums, keep, *attended_t)
    after = [keep, *attended_t, *[block_sum.halve() for block_sum in mlp_sums]]

    dx_parts, dproj, dgain_heads = [], (), 0.0
    if not by_pair:
        (attended_got,) = sync(attended_got)
    for index in range(part_count):
        grad = attended_own if by_pair and index == 0 else attended_got
        dx, dgain, *dproj = attend_back(
            grad, kept, head_out, row_sums[index], attn_cuts, attn_chunks, tables, *gains, group, width, index, part_count, after, dproj
        )
        dgain_heads = dgain_heads + dgain
        if by_pair and index == 0:
            dx, attended_got, ffn_parts[1] = arrive(mlp_sums, dx, attended_got, ffn_parts[1])
            ffn_first = start_rows(ffn_parts[1][:half])
        elif by_pair:
            dx, ffn_first = arrive(mlp_sums, dx, ffn_first)
            ffn_rest = start_rows(ffn_parts[1][half:])
        else:
            (dx,) = arrive(mlp_sums, dx)
            ffn_rest = start_sum(ffn_parts)
        dx_parts.append(dx)
        after = [block_sum.halve() for block_sum in mlp_sums]
    dx_got = start_sum(dx_parts)
    if by_pair:
        attended_t = turn(places, [attended_got], 1, part_count, after, attended_t, 10**9)
    else:
        attended_t = turn(places, [attended_got], 0, 1, after)
    dgain_attn = sum(
        jnp.sum(array.astype(F32) * dx.astype(F32), axis=0) for array, dx in zip(normed, dx_parts)
    ) / gain_attn
    sums = jnp.concatenate([dgain_attn, dgain_mlp, dgain_heads[0], dgain_heads[1]]).reshape(-1, 128)
    hops = [("dp", dp_size, 1 << bit) for bit in range(dp_size.bit_length() - 1)]
    hops += [("tensor", tensor_size, 1 << bit) for bit in range(tensor_size.bit_length() - 1)]
    attn_sums, after = [], [*after, sums]
    for index, cut in enumerate(attn_cuts):
        sums_got = exchange(sums, *hops.pop(0))
        keep, send, token = weight_grads(*normed_t, *attended_t, *dproj, head_out, heads, *cut, after, index > 0)
        attn_sums.append(BlockSum(dp_size, keep, send, orders[index]))
        token, sums_got, ffn_rest = arrive(mlp_sums[index : index + 1], token, sums_got, ffn_rest)
        sums = sums + sums_got
        after = [token, sums]
    ffn_got = jnp.concatenate([ffn_first, ffn_rest], axis=0) if by_pair else ffn_rest

    sums_got = exchange(sums, *hops.pop(0))
    (sums_got,) = arrive(attn_sums, sums_got)
    sums = sums + sums_got
    sent = [block_sum.halve() for block_sum in attn_sums]
    sums_got = exchange(sums, *hops.pop(0))
    (sums_got,) = arrive(attn_sums, sums_got)
    sums = sums + sums_got
    sent = [block_sum.halve() for block_sum in attn_sums]
    dx_got, *_ = sync(dx_got, *sent)
    grad_normed = add_sum(dx_parts, dx_got)
    grad_inputs = (grad_middle + norm_back(unit_in, scale_in, grad_normed * gain_attn)).astype(BF16)
    grad_inputs, sums = arrive(attn_sums, grad_inputs, sums)
    while any(block_sum.flips for block_sum in attn_sums):
        for block_sum in attn_sums:
            block_sum.halve()
    for hop in hops:
        sums = sums + exchange(sums, *hop)
    sums = sums.reshape(-1)
    layer_out = add_sum(ffn_parts, ffn_got, middle).astype(BF16)
    while any(block_sum.flips for block_sum in mlp_sums):
        for block_sum in mlp_sums:
            block_sum.halve()
    mlp_parts = jnp.concatenate([block_sum.finish() for block_sum in mlp_sums], axis=1)
    attn_parts = jnp.concatenate([block_sum.finish() for block_sum in attn_sums], axis=1)
    query_part, keys_part, values_part, output_part = unpack(
        attn_parts, heads, [w_query.shape[1], key_weight.shape[1], value_weight.shape[1], w_output.shape[0]]
    )
    gate_part, up_part, down_part = unpack(mlp_parts, steps, [hidden, hidden, hidden])
    return (
        layer_out,
        grad_inputs,
        query_part,
        keys_part,
        values_part,
        output_part.T,
        gate_part,
        up_part,
        down_part.T,
        sums[:model],
        sums[model : 2 * model],
        sums[2 * model : 2 * model + width],
        sums[2 * model + width :],
    )


def solution(mesh):
    rows = P(("dp", "tensor"), None)
    wide, tall = P("dp", "tensor"), P("tensor", "dp")
    return jax.shard_map(
        functools.partial(body, mesh.shape["dp"], mesh.shape["tensor"]),
        mesh=mesh,
        in_specs=(rows, rows, wide, wide, wide, tall, wide, wide, tall, P(), P(), P(), P()),
        out_specs=(rows, rows, wide, wide, wide, tall, wide, wide, tall, P(), P(), P(), P()),
        check_vma=False,
    )
```

```python
import functools

import jax
import jax.numpy as jnp
import numpy as np
from jax import lax
from jax.experimental import pallas as pl
from jax.experimental.pallas import tpu as pltpu
from jax.sharding import PartitionSpec as P

SEQ = 512
EPSILON = 1e-06
THETA = 1000000.0
F32 = jnp.float32
BF16 = jnp.bfloat16
VMEM_LIMIT = 56 * 1024 * 1024
QUERY_TILE = 256
KEY_TILE = 128


def dot(left, right):
    return lax.dot_general(left, right, (((1,), (0,)), ((), ())), preferred_element_type=F32)


def dot_t(left, right):
    return lax.dot_general(left, right, (((1,), (1,)), ((), ())), preferred_element_type=F32)


def whole(array):
    dims = array.shape
    return pl.BlockSpec(dims, lambda *_: (0,) * len(dims))


def columns(array, count, first=0):
    return pl.BlockSpec((array.shape[0], array.shape[1] // count), lambda j: (0, first + j))


def kernel_call(kernel, name, grid, inputs, outputs, scratch, flops, after=(), into=(), into_index=0):
    after = [*into, *after]
    known = len(inputs)

    def run(*refs):
        kernel(*refs[:known], *refs[known + len(after) :])

    moved = sum(array.size * array.dtype.itemsize for array, _ in inputs)
    return pl.pallas_call(
        run,
        grid=grid,
        in_specs=[spec for _, spec in inputs] + [pl.BlockSpec(memory_space=pl.ANY)] * len(after),
        out_specs=[spec for _, _, spec in outputs],
        out_shape=[jax.ShapeDtypeStruct(shape, dtype) for shape, dtype, _ in outputs],
        scratch_shapes=scratch,
        input_output_aliases={known + index: into_index + index for index in range(len(into))},
        compiler_params=pltpu.CompilerParams(vmem_limit_bytes=VMEM_LIMIT),
        cost_estimate=pl.CostEstimate(flops=64 * flops, bytes_accessed=64 * moved if flops else 1, transcendentals=0),
        name=name,
    )(*[array for array, _ in inputs], *after)


def sync(*arrays):
    spec = pl.BlockSpec(memory_space=pl.ANY)
    return kernel_call(
        lambda *_: None, "sync", (), [], [(array.shape, array.dtype, spec) for array in arrays], [], 0, (), arrays
    )


def rope_tables(width):
    half = width // 2
    places = np.arange(SEQ, dtype=np.float32)
    inverse = (THETA ** (-2.0 * np.arange(half, dtype=np.float32) / width)).astype(np.float32)
    angles = places[:, None] * inverse[None, :]
    cosine = np.concatenate([np.cos(angles), np.cos(angles)], axis=-1)
    sine = np.concatenate([-np.sin(angles), np.sin(angles)], axis=-1)
    return cosine.astype(np.float32), sine.astype(np.float32)


def rope(values, cosine, sine):
    half = values.shape[-1] // 2
    return values * cosine + pltpu.roll(values, half, 1) * sine


def rope_back(values, cosine, sine):
    half = values.shape[-1] // 2
    return values * cosine + pltpu.roll(values * sine, half, 1)


def score_tiles():
    for query in range(0, SEQ, QUERY_TILE):
        for key in range(0, query + QUERY_TILE, KEY_TILE):
            yield slice(key, key + KEY_TILE), slice(query, query + QUERY_TILE)


def exponents_t(keys_rot, query_rot, factor, keys, queries):
    result = jnp.exp2(dot_t(keys_rot, query_rot) * factor)
    if keys.stop - 1 <= queries.start:
        return result
    key_place = lax.broadcasted_iota(jnp.int32, result.shape, 0) + keys.start
    query_place = lax.broadcasted_iota(jnp.int32, result.shape, 1) + queries.start
    return jnp.where(key_place <= query_place, result, 0.0)


def load_weights(cuts, chunks, weight_ref):
    step = pl.program_id(0)
    for index, (first, count) in enumerate(cuts):
        places_ref, *halves = chunks[3 * index : 3 * index + 3]

        @pl.when((step >= first) & (step < first + count))
        def _():
            blocks = places_ref.shape[0]
            block = weight_ref.shape[0] // blocks
            for position in range(blocks):
                half, inner = halves[2 * position // blocks], position % (blocks // 2)
                place = pl.ds(pl.multiple_of(places_ref[position] * block, block), block)
                weight_ref[place, :] = half[inner * block : (inner + 1) * block, :]


def weight_inputs(cuts, chunks):
    inputs = []
    for (first, count), (places, *halves) in zip(cuts, chunks):
        inputs.append((places, pl.BlockSpec(memory_space=pltpu.SMEM)))
        for half in halves:
            spec = pl.BlockSpec(
                (half.shape[0], half.shape[1] // count),
                lambda j, first=first, count=count: (0, jnp.clip(j - first, 0, count - 1)),
            )
            inputs.append((half, spec))
    return inputs


def attend_kernel(group, width, cuts, normed_ref, cos_ref, sin_ref, gain_q_ref, gain_k_ref, *refs):
    chunks, (part_ref, sums_ref, kept_ref, out_ref, total, weight_ref) = refs[: 3 * len(cuts)], refs[3 * len(cuts) :]
    step = pl.program_id(0)
    load_weights(cuts, chunks, weight_ref)
    rows = normed_ref.shape[0]
    wide = group * width
    factor = float(width**-0.5 * np.log2(np.e))
    proj = dot(normed_ref[...], weight_ref[:, : wide + 2 * width])
    kept_ref[:, : wide + width] = proj[:, : wide + width].astype(BF16)
    values = proj[:, wide + width :].astype(BF16)
    kept_ref[:, 2 * (wide + width) :] = values
    for seq in range(rows // SEQ):
        place = slice(seq * SEQ, (seq + 1) * SEQ)
        rotated = []
        for head in range(group + 1):
            raw = proj[place, head * width : (head + 1) * width]
            scale = lax.rsqrt(jnp.mean(raw * raw, axis=-1, keepdims=True) + EPSILON)
            gain = gain_q_ref[...] if head < group else gain_k_ref[...]
            turned = rope(raw * scale * gain, cos_ref[...], sin_ref[...]).astype(BF16)
            kept_ref[place, wide + width + head * width : wide + width + (head + 1) * width] = turned
            rotated.append(turned)
        values_t = values[place].T
        for head in range(group):
            out_t, sums = {}, {}
            for keys, queries in score_tiles():
                exponents = exponents_t(rotated[group][keys], rotated[head][queries], factor, keys, queries)
                start = queries.start
                sums[start] = sums.get(start, 0.0) + jnp.sum(exponents, axis=0, keepdims=True)
                out_t[start] = out_t.get(start, 0.0) + dot(values_t[:, keys], exponents.astype(BF16))
            for start in out_t:
                scale = 1.0 / sums[start]
                spot = slice(seq * SEQ + start, seq * SEQ + start + QUERY_TILE)
                sums_ref[head : head + 1, spot] = scale
                out_ref[spot, head * width : (head + 1) * width] = (out_t[start] * scale).T.astype(BF16)
    out = dot_t(out_ref[...], weight_ref[:, wide + 2 * width :])

    @pl.when(step == 0)
    def _():
        total[...] = out

    @pl.when(step > 0)
    def _():
        total[...] += out

    @pl.when(step == pl.num_programs(0) - 1)
    def _():
        part_ref[...] = total[...].astype(BF16)


def part_rows(rows, width, steps, part, parts):
    return (parts * rows, width), BF16, pl.BlockSpec((rows, width // steps), lambda j: (part, j))


def attend(normed, cuts, chunks, tables, gain_q, gain_k, group, width, part, parts, after=(), into=()):
    rows, model = normed.shape
    heads = sum(count for _, count in cuts)
    block = (2 * group + 2) * width
    return kernel_call(
        functools.partial(attend_kernel, group, width, cuts),
        "attend",
        (heads,),
        [(array, whole(array)) for array in (normed, *tables, gain_q, gain_k)] + weight_inputs(cuts, chunks),
        [
            (normed.shape, BF16, whole(normed)),
            ((8 * heads, rows), F32, pl.BlockSpec((8, rows), lambda j: (j, 0))),
            part_rows(rows, heads * (2 * group + 3) * width, heads, part, parts),
            part_rows(rows, heads * group * width, heads, part, parts),
        ],
        [pltpu.VMEM((rows, model), F32), pltpu.VMEM((model, block), BF16)],
        heads * (2 * rows * model * block + 4 * rows * SEQ * group * width),
        after,
        into,
        2,
    )


def turn_kernel(places_ref, *refs):
    target_ref = refs[-1]
    count = places_ref.shape[0]
    block = target_ref.shape[0] // count
    together = max(1, min(count, 128 // block))
    begin = 0
    for source_ref in refs[:-1]:
        rows = source_ref.shape[0]
        for first in range(0, count, together):
            turned = source_ref[:, first * block : (first + together) * block].T
            for index in range(together):
                place = pl.ds(pl.multiple_of(places_ref[first + index] * block, block), block)
                target_ref[place, begin : begin + rows] = turned[index * block : (index + 1) * block]
        begin += rows


def turn(places, sources, part, parts, after=(), into=(), flops=0):
    rows, model = sources[0].shape
    width = rows * len(sources)
    return kernel_call(
        turn_kernel,
        "turn",
        (1,),
        [(places, pl.BlockSpec(memory_space=pltpu.SMEM))] + [(source, whole(source)) for source in sources],
        [((model, rows * parts), BF16, pl.BlockSpec((model, width), lambda j: (0, part // len(sources))))],
        [],
        flops,
        after,
        into,
    )


def mlp_kernel(cuts, normed_ref, grad_ref, gain_ref, *refs):
    chunks = refs[: 3 * len(cuts)]
    out_ref, dx_ref, dgain_ref, both_ref, hidden_ref, out_total, dx_total, weight_ref = refs[3 * len(cuts) :]
    step = pl.program_id(0)
    units = weight_ref.shape[1] // 3
    load_weights(cuts, chunks, weight_ref)

    @pl.when(step == 0)
    def _():
        out_total[...] = jnp.zeros_like(out_total)
        dx_total[...] = jnp.zeros_like(dx_total)

    both = dot(normed_ref[...], weight_ref[:, : 2 * units])
    gate, up = both[:, :units], both[:, units:]
    sig = 1.0 / (1.0 + jnp.exp(-gate))
    silu = gate * sig
    hidden = (silu * up).astype(BF16)
    grad_hidden = dot(grad_ref[...], weight_ref[:, 2 * units :])
    both_ref[:, :units] = (grad_hidden * up * (sig + silu * (1.0 - sig))).astype(BF16)
    both_ref[:, units:] = (grad_hidden * silu).astype(BF16)
    hidden_ref[...] = hidden
    out_total[...] += dot_t(hidden, weight_ref[:, 2 * units :])
    dx_total[...] += dot_t(both_ref[...], weight_ref[:, : 2 * units])

    @pl.when(step == pl.num_programs(0) - 1)
    def _():
        out_ref[...] = out_total[...].astype(BF16)
        dx_ref[...] = dx_total[...].astype(BF16)
        dgain_ref[...] = (
            jnp.sum(normed_ref[...].astype(F32) * dx_total[...], axis=0, keepdims=True) / gain_ref[...]
        )


def mlp(normed, grad_rows, gain, cuts, chunks, part, parts, after=(), into=()):
    rows, model = normed.shape
    steps = sum(count for _, count in cuts)
    units = chunks[0][1].shape[1] // cuts[0][1] // 3
    return kernel_call(
        functools.partial(mlp_kernel, cuts),
        "mlp",
        (steps,),
        [(array, whole(array)) for array in (normed, grad_rows, gain)] + weight_inputs(cuts, chunks),
        [
            (normed.shape, BF16, whole(normed)),
            (normed.shape, BF16, whole(normed)),
            (gain.shape, F32, whole(gain)),
            part_rows(rows, steps * 2 * units, steps, part, parts),
            part_rows(rows, steps * units, steps, part, parts),
        ],
        [pltpu.VMEM((rows, model), F32), pltpu.VMEM((rows, model), F32), pltpu.VMEM((model, 3 * units), BF16)],
        12 * rows * model * steps * units,
        after,
        into,
        3,
    )


def weight_grads_kernel(in_t, out_t, into, outof, *halves):
    wide = into.shape[1]
    half = in_t.shape[0] // 2
    *halves, token_ref = halves
    token_ref[...] = jnp.zeros_like(token_ref)
    for ref, place in zip(halves, (slice(0, half), slice(half, 2 * half))):
        ref[:, :wide] = dot(in_t[place, :], into[...]).astype(BF16)
        ref[:, wide:] = dot(out_t[place, :], outof[...]).astype(BF16)


def weight_grads(in_t, out_t, into, outof, steps, first, count, after=(), hides=True):
    model, rows = in_t.shape
    token = jax.ShapeDtypeStruct((8, 128), F32)
    target = jax.ShapeDtypeStruct((model // 2, count * (into.shape[1] + outof.shape[1]) // steps), BF16)
    return kernel_call(
        weight_grads_kernel,
        "weight_grads",
        (count,),
        [(in_t, whole(in_t)), (out_t, whole(out_t))]
        + [(array, columns(array, steps, first)) for array in (into, outof)],
        [(target.shape, BF16, columns(target, count))] * 2 + [(token.shape, F32, whole(token))],
        [],
        4 * rows * target.size if hides else 0,
        after,
    )


def attend_back_kernel(
    group, width, cuts, grad_ref, kept, out_ref, sums_ref, cos_ref, sin_ref, gain_q_ref, gain_k_ref, *refs
):
    chunks = refs[: 3 * len(cuts)]
    dx_ref, dgain_ref, dproj, total, weight_ref = refs[3 * len(cuts) :]
    step = pl.program_id(0)
    load_weights(cuts, chunks, weight_ref)
    wide = group * width
    scaling = float(width**-0.5)
    factor = float(width**-0.5 * np.log2(np.e))
    rot = wide + width
    base = 2 * rot

    @pl.when(step == 0)
    def _():
        total[...] = jnp.zeros_like(total)
        dgain_ref[...] = jnp.zeros_like(dgain_ref)

    def head_back(place, head, cotangent):
        gain = gain_q_ref[...] if head < group else gain_k_ref[...]
        raw = kept[place, head * width : (head + 1) * width].astype(F32)
        scale = lax.rsqrt(jnp.mean(raw * raw, axis=-1, keepdims=True) + EPSILON)
        unit = raw * scale
        cot = rope_back(cotangent * scaling, cos_ref[...], sin_ref[...])
        row = 0 if head < group else 1
        dgain_ref[row : row + 1, :] += jnp.sum(cot * unit, axis=0, keepdims=True)
        cot = cot * gain
        result = scale * (cot - unit * jnp.mean(unit * cot, axis=-1, keepdims=True))
        dproj[place, head * width : (head + 1) * width] = result.astype(BF16)

    grad_heads = dot(grad_ref[...], weight_ref[:, wide + 2 * width :]).astype(BF16)
    for seq in range(grad_heads.shape[0] // SEQ):
        place = slice(seq * SEQ, (seq + 1) * SEQ)
        keys_rot = kept[place, rot + wide : rot + wide + width]
        keys_t = keys_rot.T
        values = kept[place, base : base + width]
        dkeys, dvalues = [{key: 0.0 for key in range(0, SEQ, KEY_TILE)} for _ in range(2)]
        for head in range(group):
            query_rot = kept[place, rot + head * width : rot + (head + 1) * width]
            grad_head = grad_heads[place, head * width : (head + 1) * width]
            weighted = grad_head.astype(F32) * out_ref[place, head * width : (head + 1) * width].astype(F32)
            inner = jnp.sum(weighted.T, axis=0, keepdims=True)
            scale = sums_ref[head : head + 1, place]
            dqueries = {}
            for keys, queries in score_tiles():
                exponents = exponents_t(keys_rot[keys], query_rot[queries], factor, keys, queries)
                probs = exponents * scale[:, queries]
                dprobs = dot_t(values[keys], grad_head[queries])
                dscores = (probs * (dprobs - inner[:, queries])).astype(BF16)
                dvalues[keys.start] += dot(probs.astype(BF16), grad_head[queries])
                dkeys[keys.start] += dot(dscores, query_rot[queries])
                start = queries.start
                dqueries[start] = dqueries.get(start, 0.0) + dot(keys_t[:, keys], dscores)
            head_back(place, head, jnp.concatenate([dqueries[start].T for start in dqueries], axis=0))
        dkeys = jnp.concatenate(list(dkeys.values()), axis=0)
        dvalues = jnp.concatenate(list(dvalues.values()), axis=0)
        head_back(place, group, dkeys)
        dproj[place, wide + width :] = dvalues.astype(BF16)
    total[...] += dot_t(dproj[...], weight_ref[:, : wide + 2 * width])

    @pl.when(step == pl.num_programs(0) - 1)
    def _():
        dx_ref[...] = total[...].astype(BF16)


def attend_back(grad, kept, head_out, sums, cuts, chunks, tables, gain_q, gain_k, group, width, part, parts, after=(), into=()):
    rows, model = grad.shape
    heads = sum(count for _, count in cuts)
    block = (2 * group + 2) * width
    return kernel_call(
        functools.partial(attend_back_kernel, group, width, cuts),
        "attend_back",
        (heads,),
        [
            (grad, whole(grad)),
            (kept, pl.BlockSpec((rows, kept.shape[1] // heads), lambda j: (part, j))),
            (head_out, pl.BlockSpec((rows, head_out.shape[1] // heads), lambda j: (part, j))),
            (sums, pl.BlockSpec((8, rows), lambda j: (j, 0))),
            *[(array, whole(array)) for array in (*tables, gain_q, gain_k)],
            *weight_inputs(cuts, chunks),
        ],
        [
            (grad.shape, BF16, whole(grad)),
            ((8, width), F32, pl.BlockSpec((8, width), lambda j: (0, 0))),
            part_rows(rows, heads * (group + 2) * width, heads, part, parts),
        ],
        [pltpu.VMEM((rows, model), F32), pltpu.VMEM((model, block), BF16)],
        heads * (2 * rows * model * block + 10 * rows * SEQ * group * width),
        after,
        into,
        2,
    )


def unit_rows(values):
    scale = lax.rsqrt(jnp.mean(values * values, axis=-1, keepdims=True) + EPSILON)
    return values * scale, scale


def norm_back(unit, scale, cotangent):
    return scale * (cotangent - unit * jnp.mean(unit * cotangent, axis=-1, keepdims=True))


def pack(parts, pieces):
    rows = parts[0].shape[0]
    split = [part.reshape(rows, pieces, part.shape[1] // pieces) for part in parts]
    return jnp.concatenate(split, axis=2).reshape(rows, -1)


def unpack(packed, pieces, widths):
    rows = packed.shape[0]
    split = packed.reshape(rows, pieces, -1).astype(F32)
    ends = np.cumsum([width // pieces for width in widths])
    return [
        split[:, :, end - width // pieces : end].reshape(rows, width) for end, width in zip(ends, widths)
    ]


def relative_places(size):
    relative = jnp.arange(size, dtype=jnp.int32) ^ lax.axis_index("dp")
    layers = size // 4
    return (relative & 1) * (2 * layers) + ((relative >> 1) & 1) * layers + (relative >> 2)


def exchange(array, axis, size, flip):
    return lax.ppermute(array, axis, [(index, index ^ flip) for index in range(size)])


def z_bits(size):
    return [4 << bit for bit in reversed(range((size // 4).bit_length() - 1))]


class BlockGather:
    def __init__(self, size, block, flips):
        self.size, self.flips = size, list(flips)
        self.held, self.done, self.got = block, 0, None

    def start(self):
        self.got = exchange(self.held, "dp", self.size, self.flips[self.done])
        self.done += 1

    def join(self):
        self.held = jnp.concatenate([self.held, self.got], axis=0)

    def chunk(self):
        position = jnp.arange(self.size, dtype=jnp.int32)
        place = lax.axis_index("dp") ^ sum(
            ((position >> bit) & 1) * flip for bit, flip in enumerate(self.flips)
        )
        return place, self.held, self.got


class BlockSum:
    def __init__(self, size, keep, send, flips):
        self.size, self.flips = size, list(flips)
        self.bits = [2, *z_bits(size)]
        self.left = list(self.bits)
        self.shape = (2,) * len(self.bits) + (-1, keep.shape[1])
        self.terms = [(keep.reshape(self.shape), self.bits)]
        self.got = exchange(send, "dp", size, 1)

    def part(self, flip=None):
        total = 0.0
        for array, bits in self.terms:
            start = [int(bit == flip) for bit in bits] + [0, 0]
            stop = [
                int(bit == flip) + 1 if bit == flip or bit not in self.left else 2 for bit in bits
            ] + list(array.shape[-2:])
            piece = lax.slice(array, start, stop)
            total = total + piece.reshape((2,) * (len(self.left) - (flip is not None)) + piece.shape[-2:]).astype(F32)
        return total

    def take(self):
        if len(self.terms) == 1:
            self.got = self.got.reshape(self.shape)
        self.terms.append((self.got, list(self.left)))

    def halve(self):
        self.take()
        flip = self.flips.pop(0)
        sent = self.part(flip).astype(BF16)
        self.left.remove(flip)
        self.got = exchange(sent, "dp", self.size, flip)
        return sent

    def finish(self):
        self.take()
        return self.part()


def arrive(movers, *others):
    results = sync(*[mover.got for mover in movers], *others)
    for mover, got in zip(movers, results):
        mover.got = got
    return results[len(movers) :]


def body(
    dp_size,
    tensor_size,
    inputs,
    grad_out,
    w_query,
    key_weight,
    value_weight,
    w_output,
    w_gate,
    w_up,
    w_down,
    gain_attn,
    gain_mlp,
    gain_query,
    gain_keys,
):
    own_rows, model = inputs.shape
    width = gain_query.shape[0]
    heads = key_weight.shape[1] // width
    group = w_query.shape[1] // key_weight.shape[1]
    hidden = w_gate.shape[1]
    steps = max(1, hidden // 256)
    by_pair = tensor_size == 2 and own_rows % SEQ == 0
    part_count = 2 if by_pair else 1

    def start_rows(own):
        if by_pair:
            return exchange(own, "tensor", 2, 1)
        return lax.all_gather(own, "tensor", axis=0, tiled=True)

    def all_rows(own, got):
        return [own, got] if by_pair else [got]

    def start_sum(parts):
        if by_pair:
            return exchange(parts[1], "tensor", 2, 1)
        return lax.psum_scatter(parts[0], "tensor", scatter_dimension=0, tiled=True)

    def add_sum(parts, got, base=0.0):
        total = base + got.astype(F32)
        return total + parts[0].astype(F32) if by_pair else total

    tables = rope_tables(width)
    gains = gain_query[None, :], gain_keys[None, :]
    places = relative_places(dp_size)
    z_flips = z_bits(dp_size)
    x_flip, z_flip, z_first = 2, z_flips[-1], z_flips[:-1]

    def gather_start(packed, steps):
        first = max(1, steps // 2)
        cuts = [(0, first), (first, steps - first)] if steps > 1 else [(0, 1)]
        unit = packed.shape[1] // steps
        orders = [*z_first, z_flip, x_flip, 1], [*z_first, x_flip, z_flip, 1]
        return cuts, [
            BlockGather(dp_size, packed[:, start * unit : (start + count) * unit], flips)
            for (start, count), flips in zip(cuts, orders)
        ]

    attn_cuts, attn_gathers = gather_start(pack([w_query, key_weight, value_weight, w_output.T], heads), heads)
    inputs_f = inputs.astype(F32)
    unit_in, scale_in = unit_rows(inputs_f)
    normed_own = (unit_in * gain_attn).astype(BF16)
    for gather in attn_gathers:
        gather.start()
    grad_t = turn(places, [grad_out], 0, part_count) if by_pair else ()
    normed_t = turn(places, [normed_own], 0, part_count) if by_pair else ()
    half = own_rows // 2
    grad_half = start_rows(grad_out[:half]) if by_pair else start_rows(grad_out)
    grad_half, packed, *turned = arrive(
        attn_gathers, grad_half, pack([w_gate, w_up, w_down.T], steps), *grad_t, *normed_t
    )
    grad_t, normed_t = turned[:1], turned[1:]

    mlp_cuts, mlp_gathers = gather_start(packed, steps)
    while attn_gathers[0].done < len(attn_gathers[0].flips) - 2:
        for gather in attn_gathers:
            gather.join()
            gather.start()
        arrive(attn_gathers)
    for gather in attn_gathers:
        gather.join()
        gather.start()
    for gather in mlp_gathers:
        gather.start()
    normed_got = start_rows(normed_own)
    (normed_got,) = arrive([*attn_gathers, *mlp_gathers], normed_got)
    normed = all_rows(normed_own, normed_got)
    for gather in attn_gathers:
        gather.join()
        gather.start()
    arrive(attn_gathers)
    attn_chunks = [gather.chunk() for gather in attn_gathers]

    def grow_mlp():
        sent = []
        if mlp_gathers[0].done < len(mlp_gathers[0].flips):
            for gather in mlp_gathers:
                gather.join()
                gather.start()
                sent.append(gather.held)
        return sent

    parts, row_sums, kept = [None] * part_count, [None] * part_count, ()
    grad_rest = start_rows(grad_out[half:]) if by_pair else None
    for index in reversed(range(part_count)):
        after = grow_mlp()
        parts[index], row_sums[index], *kept = attend(
            normed[index], attn_cuts, attn_chunks, tables, *gains, group, width, index, part_count, after, kept
        )
        if index == part_count - 1:
            if by_pair:
                parts[index], grad_rest = arrive(mlp_gathers, parts[index], grad_rest)
            else:
                (parts[index],) = arrive(mlp_gathers, parts[index])
            part_got = start_sum(parts)
    parts[0], part_got = arrive(mlp_gathers, parts[0], part_got)
    kept, head_out = kept
    while mlp_gathers[0].done < len(mlp_gathers[0].flips):
        grow_mlp()
        arrive(mlp_gathers)
    mlp_chunks = [gather.chunk() for gather in mlp_gathers]
    grad_rows = [grad_out, jnp.concatenate([grad_half, grad_rest], axis=0)] if by_pair else [grad_half]
    middle = add_sum(parts, part_got, inputs_f)
    unit_mid, scale_mid = unit_rows(middle)
    normed_own = (unit_mid * gain_mlp).astype(BF16)
    normed_got = start_rows(normed_own)

    def run_mlp(index, array, after, into):
        return mlp(
            array, grad_rows[index], gain_mlp[None, :], mlp_cuts, mlp_chunks, index, part_count, after, into
        )

    if by_pair:
        ffn, dx, dgain, *kept_mlp = run_mlp(0, normed_own, [normed_own], ())
        grad_t = turn(places, grad_rows[1:], 1, part_count, [dx], grad_t)
        normed_t = turn(places, normed[1:], 1, part_count, grad_t, normed_t)
        dx, normed_got, *turned = sync(dx, normed_got, *grad_t, *normed_t)
        grad_t, normed_t = turned[:1], turned[1:]
        ffn_parts, dx_parts, dgain_mlp = [ffn], [dx], dgain[0]
        ffn, dx, dgain, *kept_mlp = run_mlp(1, normed_got, [dx], kept_mlp)
        ffn_parts.append(ffn)
        dx_parts.append(dx)
        dgain_mlp = dgain_mlp + dgain[0]
        after = [dx]
    else:
        grad_t = turn(places, grad_rows, 0, 1)
        normed_t = turn(places, normed, 0, 1)
        ffn, dx, dgain, *kept_mlp = run_mlp(0, normed_got, (), ())
        ffn_parts, dx_parts, dgain_mlp = [ffn], [dx], dgain[0]
        after = [dx]
    normed_mlp_t = turn(places, all_rows(normed_own, normed_got), 0, part_count, after, flops=10**9)

    dx_got = start_sum(dx_parts)
    orders = [x_flip, z_flip, *z_first], [z_flip, x_flip, *z_first]

    def mlp_weight_grads(index, after):
        keep, send, token = weight_grads(
            *normed_mlp_t, *grad_t, *kept_mlp, steps, *mlp_cuts[index], after, index > 0
        )
        return token, BlockSum(dp_size, keep, send, orders[index])

    keep, block_sum = mlp_weight_grads(0, after)
    mlp_sums = [block_sum]
    keep, dx_got = sync(keep, dx_got)
    grad_middle = grad_out.astype(F32) + norm_back(unit_mid, scale_mid, add_sum(dx_parts, dx_got) * gain_mlp)
    attended_own = grad_middle.astype(BF16)
    attended_got = start_rows(attended_own)
    after = [attended_own]
    if len(mlp_cuts) > 1:
        keep, block_sum = mlp_weight_grads(1, after)
        mlp_sums.append(block_sum)
        after = [keep]
    attended_t = turn(places, [attended_own], 0, part_count, after) if by_pair else ()
    keep, *attended_t = arrive(mlp_sums, keep, *attended_t)
    after = [keep, *attended_t, *[block_sum.halve() for block_sum in mlp_sums]]

    dx_parts, dproj, dgain_heads = [], (), 0.0
    if not by_pair:
        (attended_got,) = sync(attended_got)
    for index in range(part_count):
        grad = attended_own if by_pair and index == 0 else attended_got
        dx, dgain, *dproj = attend_back(
            grad, kept, head_out, row_sums[index], attn_cuts, attn_chunks, tables, *gains, group, width, index, part_count, after, dproj
        )
        dgain_heads = dgain_heads + dgain
        if by_pair and index == 0:
            dx, attended_got, ffn_parts[1] = arrive(mlp_sums, dx, attended_got, ffn_parts[1])
            ffn_first = start_rows(ffn_parts[1][:half])
        elif by_pair:
            dx, ffn_first = arrive(mlp_sums, dx, ffn_first)
            ffn_rest = start_rows(ffn_parts[1][half:])
        else:
            (dx,) = arrive(mlp_sums, dx)
            ffn_rest = start_sum(ffn_parts)
        dx_parts.append(dx)
        after = [block_sum.halve() for block_sum in mlp_sums]
    dx_got = start_sum(dx_parts)
    if by_pair:
        attended_t = turn(places, [attended_got], 1, part_count, after, attended_t, 10**9)
    else:
        attended_t = turn(places, [attended_got], 0, 1, after)
    dgain_attn = sum(
        jnp.sum(array.astype(F32) * dx.astype(F32), axis=0) for array, dx in zip(normed, dx_parts)
    ) / gain_attn
    sums = jnp.concatenate([dgain_attn, dgain_mlp, dgain_heads[0], dgain_heads[1]]).reshape(-1, 128)
    hops = [("dp", dp_size, 1 << bit) for bit in range(dp_size.bit_length() - 1)]
    hops += [("tensor", tensor_size, 1 << bit) for bit in range(tensor_size.bit_length() - 1)]
    attn_sums, after = [], [*after, sums]
    for index, cut in enumerate(attn_cuts):
        sums_got = exchange(sums, *hops.pop(0))
        keep, send, token = weight_grads(*normed_t, *attended_t, *dproj, head_out, heads, *cut, after, index > 0)
        attn_sums.append(BlockSum(dp_size, keep, send, orders[index]))
        token, sums_got, ffn_rest = arrive([] if index else mlp_sums[:1], token, sums_got, ffn_rest)
        sums = sums + sums_got
        after = [token, sums]
    ffn_got = jnp.concatenate([ffn_first, ffn_rest], axis=0) if by_pair else ffn_rest

    sums_got = exchange(sums, *hops.pop(0))
    (sums_got,) = arrive(attn_sums, sums_got)
    sums = sums + sums_got
    sent = [block_sum.halve() for block_sum in attn_sums]
    sums_got = exchange(sums, *hops.pop(0))
    (sums_got,) = arrive([*attn_sums, *mlp_sums[1:]], sums_got)
    sums = sums + sums_got
    sent = [block_sum.halve() for block_sum in attn_sums]
    dx_got, *_ = sync(dx_got, *sent)
    grad_normed = add_sum(dx_parts, dx_got)
    grad_inputs = (grad_middle + norm_back(unit_in, scale_in, grad_normed * gain_attn)).astype(BF16)
    (sums,) = arrive(attn_sums, sums)
    while any(block_sum.flips for block_sum in attn_sums):
        for block_sum in attn_sums:
            block_sum.halve()
    for hop in hops:
        sums = sums + exchange(sums, *hop)
    sums = sums.reshape(-1)
    layer_out = add_sum(ffn_parts, ffn_got, middle).astype(BF16)
    while any(block_sum.flips for block_sum in mlp_sums):
        for block_sum in mlp_sums:
            block_sum.halve()
    mlp_parts = jnp.concatenate([block_sum.finish() for block_sum in mlp_sums], axis=1)
    attn_parts = jnp.concatenate([block_sum.finish() for block_sum in attn_sums], axis=1)
    query_part, keys_part, values_part, output_part = unpack(
        attn_parts, heads, [w_query.shape[1], key_weight.shape[1], value_weight.shape[1], w_output.shape[0]]
    )
    gate_part, up_part, down_part = unpack(mlp_parts, steps, [hidden, hidden, hidden])
    return (
        layer_out,
        grad_inputs,
        query_part,
        keys_part,
        values_part,
        output_part.T,
        gate_part,
        up_part,
        down_part.T,
        sums[:model],
        sums[model : 2 * model],
        sums[2 * model : 2 * model + width],
        sums[2 * model + width :],
    )


def solution(mesh):
    rows = P(("dp", "tensor"), None)
    wide, tall = P("dp", "tensor"), P("tensor", "dp")
    return jax.shard_map(
        functools.partial(body, mesh.shape["dp"], mesh.shape["tensor"]),
        mesh=mesh,
        in_specs=(rows, rows, wide, wide, wide, tall, wide, wide, tall, P(), P(), P(), P()),
        out_specs=(rows, rows, wide, wide, wide, tall, wide, wide, tall, P(), P(), P(), P()),
        check_vma=False,
    )
```

```python
import functools

import jax
import jax.numpy as jnp
import numpy as np
from jax import lax
from jax.experimental import pallas as pl
from jax.experimental.pallas import tpu as pltpu
from jax.sharding import PartitionSpec as P

SEQ = 512
EPSILON = 1e-06
THETA = 1000000.0
F32 = jnp.float32
BF16 = jnp.bfloat16
VMEM_LIMIT = 56 * 1024 * 1024
QUERY_TILE = 256
KEY_TILE = 128


def dot(left, right):
    return lax.dot_general(left, right, (((1,), (0,)), ((), ())), preferred_element_type=F32)


def dot_t(left, right):
    return lax.dot_general(left, right, (((1,), (1,)), ((), ())), preferred_element_type=F32)


def whole(array):
    dims = array.shape
    return pl.BlockSpec(dims, lambda *_: (0,) * len(dims))


def columns(array, count, first=0):
    return pl.BlockSpec((array.shape[0], array.shape[1] // count), lambda j: (0, first + j))


def kernel_call(kernel, name, grid, inputs, outputs, scratch, flops, after=(), into=(), into_index=0):
    after = [*into, *after]
    known = len(inputs)

    def run(*refs):
        kernel(*refs[:known], *refs[known + len(after) :])

    moved = sum(array.size * array.dtype.itemsize for array, _ in inputs)
    return pl.pallas_call(
        run,
        grid=grid,
        in_specs=[spec for _, spec in inputs] + [pl.BlockSpec(memory_space=pl.ANY)] * len(after),
        out_specs=[spec for _, _, spec in outputs],
        out_shape=[jax.ShapeDtypeStruct(shape, dtype) for shape, dtype, _ in outputs],
        scratch_shapes=scratch,
        input_output_aliases={known + index: into_index + index for index in range(len(into))},
        compiler_params=pltpu.CompilerParams(vmem_limit_bytes=VMEM_LIMIT),
        cost_estimate=pl.CostEstimate(flops=64 * flops, bytes_accessed=64 * moved if flops else 1, transcendentals=0),
        name=name,
    )(*[array for array, _ in inputs], *after)


def sync(*arrays):
    spec = pl.BlockSpec(memory_space=pl.ANY)
    return kernel_call(
        lambda *_: None, "sync", (), [], [(array.shape, array.dtype, spec) for array in arrays], [], 0, (), arrays
    )


def rope_tables(width):
    half = width // 2
    places = np.arange(SEQ, dtype=np.float32)
    inverse = (THETA ** (-2.0 * np.arange(half, dtype=np.float32) / width)).astype(np.float32)
    angles = places[:, None] * inverse[None, :]
    cosine = np.concatenate([np.cos(angles), np.cos(angles)], axis=-1)
    sine = np.concatenate([-np.sin(angles), np.sin(angles)], axis=-1)
    return cosine.astype(np.float32), sine.astype(np.float32)


def rope(values, cosine, sine):
    half = values.shape[-1] // 2
    return values * cosine + pltpu.roll(values, half, 1) * sine


def rope_back(values, cosine, sine):
    half = values.shape[-1] // 2
    return values * cosine + pltpu.roll(values * sine, half, 1)


def score_tiles():
    for query in range(0, SEQ, QUERY_TILE):
        for key in range(0, query + QUERY_TILE, KEY_TILE):
            yield slice(key, key + KEY_TILE), slice(query, query + QUERY_TILE)


def exponents_t(keys_rot, query_rot, factor, keys, queries):
    result = jnp.exp2(dot_t(keys_rot, query_rot) * factor)
    if keys.stop - 1 <= queries.start:
        return result
    key_place = lax.broadcasted_iota(jnp.int32, result.shape, 0) + keys.start
    query_place = lax.broadcasted_iota(jnp.int32, result.shape, 1) + queries.start
    return jnp.where(key_place <= query_place, result, 0.0)


def load_weights(cuts, chunks, weight_ref):
    step = pl.program_id(0)
    for index, (first, count) in enumerate(cuts):
        places_ref, *halves = chunks[3 * index : 3 * index + 3]

        @pl.when((step >= first) & (step < first + count))
        def _():
            blocks = places_ref.shape[0]
            block = weight_ref.shape[0] // blocks
            for position in range(blocks):
                half, inner = halves[2 * position // blocks], position % (blocks // 2)
                place = pl.ds(pl.multiple_of(places_ref[position] * block, block), block)
                weight_ref[place, :] = half[inner * block : (inner + 1) * block, :]


def weight_inputs(cuts, chunks):
    inputs = []
    for (first, count), (places, *halves) in zip(cuts, chunks):
        inputs.append((places, pl.BlockSpec(memory_space=pltpu.SMEM)))
        for half in halves:
            spec = pl.BlockSpec(
                (half.shape[0], half.shape[1] // count),
                lambda j, first=first, count=count: (0, jnp.clip(j - first, 0, count - 1)),
            )
            inputs.append((half, spec))
    return inputs


def attend_kernel(group, width, cuts, normed_ref, cos_ref, sin_ref, gain_q_ref, gain_k_ref, *refs):
    chunks, (part_ref, sums_ref, kept_ref, out_ref, total, weight_ref) = refs[: 3 * len(cuts)], refs[3 * len(cuts) :]
    step = pl.program_id(0)
    load_weights(cuts, chunks, weight_ref)
    rows = normed_ref.shape[0]
    wide = group * width
    factor = float(width**-0.5 * np.log2(np.e))
    proj = dot(normed_ref[...], weight_ref[:, : wide + 2 * width])
    kept_ref[:, : wide + width] = proj[:, : wide + width].astype(BF16)
    values = proj[:, wide + width :].astype(BF16)
    kept_ref[:, 2 * (wide + width) :] = values
    for seq in range(rows // SEQ):
        place = slice(seq * SEQ, (seq + 1) * SEQ)
        rotated = []
        for head in range(group + 1):
            raw = proj[place, head * width : (head + 1) * width]
            scale = lax.rsqrt(jnp.mean(raw * raw, axis=-1, keepdims=True) + EPSILON)
            gain = gain_q_ref[...] if head < group else gain_k_ref[...]
            turned = rope(raw * scale * gain, cos_ref[...], sin_ref[...]).astype(BF16)
            kept_ref[place, wide + width + head * width : wide + width + (head + 1) * width] = turned
            rotated.append(turned)
        values_t = values[place].T
        for head in range(group):
            out_t, sums = {}, {}
            for keys, queries in score_tiles():
                exponents = exponents_t(rotated[group][keys], rotated[head][queries], factor, keys, queries)
                start = queries.start
                sums[start] = sums.get(start, 0.0) + jnp.sum(exponents, axis=0, keepdims=True)
                out_t[start] = out_t.get(start, 0.0) + dot(values_t[:, keys], exponents.astype(BF16))
            for start in out_t:
                scale = 1.0 / sums[start]
                spot = slice(seq * SEQ + start, seq * SEQ + start + QUERY_TILE)
                sums_ref[head : head + 1, spot] = scale
                out_ref[spot, head * width : (head + 1) * width] = (out_t[start] * scale).T.astype(BF16)
    out = dot_t(out_ref[...], weight_ref[:, wide + 2 * width :])

    @pl.when(step == 0)
    def _():
        total[...] = out

    @pl.when(step > 0)
    def _():
        total[...] += out

    @pl.when(step == pl.num_programs(0) - 1)
    def _():
        part_ref[...] = total[...].astype(BF16)


def part_rows(rows, width, steps, part, parts):
    return (parts * rows, width), BF16, pl.BlockSpec((rows, width // steps), lambda j: (part, j))


def attend(normed, cuts, chunks, tables, gain_q, gain_k, group, width, part, parts, after=(), into=()):
    rows, model = normed.shape
    heads = sum(count for _, count in cuts)
    block = (2 * group + 2) * width
    return kernel_call(
        functools.partial(attend_kernel, group, width, cuts),
        "attend",
        (heads,),
        [(array, whole(array)) for array in (normed, *tables, gain_q, gain_k)] + weight_inputs(cuts, chunks),
        [
            (normed.shape, BF16, whole(normed)),
            ((8 * heads, rows), F32, pl.BlockSpec((8, rows), lambda j: (j, 0))),
            part_rows(rows, heads * (2 * group + 3) * width, heads, part, parts),
            part_rows(rows, heads * group * width, heads, part, parts),
        ],
        [pltpu.VMEM((rows, model), F32), pltpu.VMEM((model, block), BF16)],
        heads * (2 * rows * model * block + 4 * rows * SEQ * group * width),
        after,
        into,
        2,
    )


def turn_kernel(places_ref, *refs):
    target_ref = refs[-1]
    count = places_ref.shape[0]
    block = target_ref.shape[0] // count
    together = max(1, min(count, 128 // block))
    begin = 0
    for source_ref in refs[:-1]:
        rows = source_ref.shape[0]
        for first in range(0, count, together):
            turned = source_ref[:, first * block : (first + together) * block].T
            for index in range(together):
                place = pl.ds(pl.multiple_of(places_ref[first + index] * block, block), block)
                target_ref[place, begin : begin + rows] = turned[index * block : (index + 1) * block]
        begin += rows


def turn(places, sources, part, parts, after=(), into=(), flops=0):
    rows, model = sources[0].shape
    width = rows * len(sources)
    return kernel_call(
        turn_kernel,
        "turn",
        (1,),
        [(places, pl.BlockSpec(memory_space=pltpu.SMEM))] + [(source, whole(source)) for source in sources],
        [((model, rows * parts), BF16, pl.BlockSpec((model, width), lambda j: (0, part // len(sources))))],
        [],
        flops,
        after,
        into,
    )


def mlp_kernel(cuts, normed_ref, grad_ref, gain_ref, *refs):
    chunks = refs[: 3 * len(cuts)]
    out_ref, dx_ref, dgain_ref, both_ref, hidden_ref, out_total, dx_total, weight_ref = refs[3 * len(cuts) :]
    step = pl.program_id(0)
    units = weight_ref.shape[1] // 3
    load_weights(cuts, chunks, weight_ref)

    @pl.when(step == 0)
    def _():
        out_total[...] = jnp.zeros_like(out_total)
        dx_total[...] = jnp.zeros_like(dx_total)

    both = dot(normed_ref[...], weight_ref[:, : 2 * units])
    gate, up = both[:, :units], both[:, units:]
    sig = 1.0 / (1.0 + jnp.exp(-gate))
    silu = gate * sig
    hidden = (silu * up).astype(BF16)
    grad_hidden = dot(grad_ref[...], weight_ref[:, 2 * units :])
    both_ref[:, :units] = (grad_hidden * up * (sig + silu * (1.0 - sig))).astype(BF16)
    both_ref[:, units:] = (grad_hidden * silu).astype(BF16)
    hidden_ref[...] = hidden
    out_total[...] += dot_t(hidden, weight_ref[:, 2 * units :])
    dx_total[...] += dot_t(both_ref[...], weight_ref[:, : 2 * units])

    @pl.when(step == pl.num_programs(0) - 1)
    def _():
        out_ref[...] = out_total[...].astype(BF16)
        dx_ref[...] = dx_total[...].astype(BF16)
        dgain_ref[...] = (
            jnp.sum(normed_ref[...].astype(F32) * dx_total[...], axis=0, keepdims=True) / gain_ref[...]
        )


def mlp(normed, grad_rows, gain, cuts, chunks, part, parts, after=(), into=()):
    rows, model = normed.shape
    steps = sum(count for _, count in cuts)
    units = chunks[0][1].shape[1] // cuts[0][1] // 3
    return kernel_call(
        functools.partial(mlp_kernel, cuts),
        "mlp",
        (steps,),
        [(array, whole(array)) for array in (normed, grad_rows, gain)] + weight_inputs(cuts, chunks),
        [
            (normed.shape, BF16, whole(normed)),
            (normed.shape, BF16, whole(normed)),
            (gain.shape, F32, whole(gain)),
            part_rows(rows, steps * 2 * units, steps, part, parts),
            part_rows(rows, steps * units, steps, part, parts),
        ],
        [pltpu.VMEM((rows, model), F32), pltpu.VMEM((rows, model), F32), pltpu.VMEM((model, 3 * units), BF16)],
        12 * rows * model * steps * units,
        after,
        into,
        3,
    )


def weight_grads_kernel(in_t, out_t, into, outof, *halves):
    wide = into.shape[1]
    half = in_t.shape[0] // 2
    *halves, token_ref = halves
    token_ref[...] = jnp.zeros_like(token_ref)
    for ref, place in zip(halves, (slice(0, half), slice(half, 2 * half))):
        ref[:, :wide] = dot(in_t[place, :], into[...]).astype(BF16)
        ref[:, wide:] = dot(out_t[place, :], outof[...]).astype(BF16)


def weight_grads(in_t, out_t, into, outof, steps, first, count, after=(), hides=True):
    model, rows = in_t.shape
    token = jax.ShapeDtypeStruct((8, 128), F32)
    target = jax.ShapeDtypeStruct((model // 2, count * (into.shape[1] + outof.shape[1]) // steps), BF16)
    return kernel_call(
        weight_grads_kernel,
        "weight_grads",
        (count,),
        [(in_t, whole(in_t)), (out_t, whole(out_t))]
        + [(array, columns(array, steps, first)) for array in (into, outof)],
        [(target.shape, BF16, columns(target, count))] * 2 + [(token.shape, F32, whole(token))],
        [],
        4 * rows * target.size if hides else 0,
        after,
    )


def attend_back_kernel(
    group, width, cuts, grad_ref, kept, out_ref, sums_ref, cos_ref, sin_ref, gain_q_ref, gain_k_ref, *refs
):
    chunks = refs[: 3 * len(cuts)]
    dx_ref, dgain_ref, dproj, total, weight_ref = refs[3 * len(cuts) :]
    step = pl.program_id(0)
    load_weights(cuts, chunks, weight_ref)
    wide = group * width
    scaling = float(width**-0.5)
    factor = float(width**-0.5 * np.log2(np.e))
    rot = wide + width
    base = 2 * rot

    @pl.when(step == 0)
    def _():
        total[...] = jnp.zeros_like(total)
        dgain_ref[...] = jnp.zeros_like(dgain_ref)

    def head_back(place, head, cotangent):
        gain = gain_q_ref[...] if head < group else gain_k_ref[...]
        raw = kept[place, head * width : (head + 1) * width].astype(F32)
        scale = lax.rsqrt(jnp.mean(raw * raw, axis=-1, keepdims=True) + EPSILON)
        unit = raw * scale
        cot = rope_back(cotangent * scaling, cos_ref[...], sin_ref[...])
        row = 0 if head < group else 1
        dgain_ref[row : row + 1, :] += jnp.sum(cot * unit, axis=0, keepdims=True)
        cot = cot * gain
        result = scale * (cot - unit * jnp.mean(unit * cot, axis=-1, keepdims=True))
        dproj[place, head * width : (head + 1) * width] = result.astype(BF16)

    grad_heads = dot(grad_ref[...], weight_ref[:, wide + 2 * width :]).astype(BF16)
    for seq in range(grad_heads.shape[0] // SEQ):
        place = slice(seq * SEQ, (seq + 1) * SEQ)
        keys_rot = kept[place, rot + wide : rot + wide + width]
        keys_t = keys_rot.T
        values = kept[place, base : base + width]
        dkeys, dvalues = [{key: 0.0 for key in range(0, SEQ, KEY_TILE)} for _ in range(2)]
        for head in range(group):
            query_rot = kept[place, rot + head * width : rot + (head + 1) * width]
            grad_head = grad_heads[place, head * width : (head + 1) * width]
            weighted = grad_head.astype(F32) * out_ref[place, head * width : (head + 1) * width].astype(F32)
            inner = jnp.sum(weighted.T, axis=0, keepdims=True)
            scale = sums_ref[head : head + 1, place]
            dqueries = {}
            for keys, queries in score_tiles():
                exponents = exponents_t(keys_rot[keys], query_rot[queries], factor, keys, queries)
                probs = exponents * scale[:, queries]
                dprobs = dot_t(values[keys], grad_head[queries])
                dscores = (probs * (dprobs - inner[:, queries])).astype(BF16)
                dvalues[keys.start] += dot(probs.astype(BF16), grad_head[queries])
                dkeys[keys.start] += dot(dscores, query_rot[queries])
                start = queries.start
                dqueries[start] = dqueries.get(start, 0.0) + dot(keys_t[:, keys], dscores)
            head_back(place, head, jnp.concatenate([dqueries[start].T for start in dqueries], axis=0))
        dkeys = jnp.concatenate(list(dkeys.values()), axis=0)
        dvalues = jnp.concatenate(list(dvalues.values()), axis=0)
        head_back(place, group, dkeys)
        dproj[place, wide + width :] = dvalues.astype(BF16)
    total[...] += dot_t(dproj[...], weight_ref[:, : wide + 2 * width])

    @pl.when(step == pl.num_programs(0) - 1)
    def _():
        dx_ref[...] = total[...].astype(BF16)


def attend_back(grad, kept, head_out, sums, cuts, chunks, tables, gain_q, gain_k, group, width, part, parts, after=(), into=()):
    rows, model = grad.shape
    heads = sum(count for _, count in cuts)
    block = (2 * group + 2) * width
    return kernel_call(
        functools.partial(attend_back_kernel, group, width, cuts),
        "attend_back",
        (heads,),
        [
            (grad, whole(grad)),
            (kept, pl.BlockSpec((rows, kept.shape[1] // heads), lambda j: (part, j))),
            (head_out, pl.BlockSpec((rows, head_out.shape[1] // heads), lambda j: (part, j))),
            (sums, pl.BlockSpec((8, rows), lambda j: (j, 0))),
            *[(array, whole(array)) for array in (*tables, gain_q, gain_k)],
            *weight_inputs(cuts, chunks),
        ],
        [
            (grad.shape, BF16, whole(grad)),
            ((8, width), F32, pl.BlockSpec((8, width), lambda j: (0, 0))),
            part_rows(rows, heads * (group + 2) * width, heads, part, parts),
        ],
        [pltpu.VMEM((rows, model), F32), pltpu.VMEM((model, block), BF16)],
        heads * (2 * rows * model * block + 10 * rows * SEQ * group * width),
        after,
        into,
        2,
    )


def unit_rows(values):
    scale = lax.rsqrt(jnp.mean(values * values, axis=-1, keepdims=True) + EPSILON)
    return values * scale, scale


def norm_back(unit, scale, cotangent):
    return scale * (cotangent - unit * jnp.mean(unit * cotangent, axis=-1, keepdims=True))


def pack(parts, pieces):
    rows = parts[0].shape[0]
    split = [part.reshape(rows, pieces, part.shape[1] // pieces) for part in parts]
    return jnp.concatenate(split, axis=2).reshape(rows, -1)


def unpack(packed, pieces, widths):
    rows = packed.shape[0]
    split = packed.reshape(rows, pieces, -1).astype(F32)
    ends = np.cumsum([width // pieces for width in widths])
    return [
        split[:, :, end - width // pieces : end].reshape(rows, width) for end, width in zip(ends, widths)
    ]


def relative_places(size):
    relative = jnp.arange(size, dtype=jnp.int32) ^ lax.axis_index("dp")
    layers = size // 4
    return (relative & 1) * (2 * layers) + ((relative >> 1) & 1) * layers + (relative >> 2)


def exchange(array, axis, size, flip):
    return lax.ppermute(array, axis, [(index, index ^ flip) for index in range(size)])


def z_bits(size):
    return [4 << bit for bit in reversed(range((size // 4).bit_length() - 1))]


class BlockGather:
    def __init__(self, size, block, flips):
        self.size, self.flips = size, list(flips)
        self.held, self.done, self.got = block, 0, None

    def start(self):
        self.got = exchange(self.held, "dp", self.size, self.flips[self.done])
        self.done += 1

    def join(self):
        self.held = jnp.concatenate([self.held, self.got], axis=0)

    def chunk(self):
        position = jnp.arange(self.size, dtype=jnp.int32)
        place = lax.axis_index("dp") ^ sum(
            ((position >> bit) & 1) * flip for bit, flip in enumerate(self.flips)
        )
        return place, self.held, self.got


class BlockSum:
    def __init__(self, size, keep, send, flips):
        self.size, self.flips = size, list(flips)
        self.bits = [2, *z_bits(size)]
        self.left = list(self.bits)
        self.shape = (2,) * len(self.bits) + (-1, keep.shape[1])
        self.terms = [(keep.reshape(self.shape), self.bits)]
        self.got = exchange(send, "dp", size, 1)

    def part(self, flip=None):
        total = 0.0
        for array, bits in self.terms:
            start = [int(bit == flip) for bit in bits] + [0, 0]
            stop = [
                int(bit == flip) + 1 if bit == flip or bit not in self.left else 2 for bit in bits
            ] + list(array.shape[-2:])
            piece = lax.slice(array, start, stop)
            total = total + piece.reshape((2,) * (len(self.left) - (flip is not None)) + piece.shape[-2:]).astype(F32)
        return total

    def take(self):
        if len(self.terms) == 1:
            self.got = self.got.reshape(self.shape)
        self.terms.append((self.got, list(self.left)))

    def halve(self):
        self.take()
        flip = self.flips.pop(0)
        sent = self.part(flip).astype(BF16)
        self.left.remove(flip)
        self.got = exchange(sent, "dp", self.size, flip)
        return sent

    def finish(self):
        self.take()
        return self.part()


def arrive(movers, *others):
    results = sync(*[mover.got for mover in movers], *others)
    for mover, got in zip(movers, results):
        mover.got = got
    return results[len(movers) :]


def body(
    dp_size,
    tensor_size,
    inputs,
    grad_out,
    w_query,
    key_weight,
    value_weight,
    w_output,
    w_gate,
    w_up,
    w_down,
    gain_attn,
    gain_mlp,
    gain_query,
    gain_keys,
):
    own_rows, model = inputs.shape
    width = gain_query.shape[0]
    heads = key_weight.shape[1] // width
    group = w_query.shape[1] // key_weight.shape[1]
    hidden = w_gate.shape[1]
    steps = max(1, hidden // 256)
    by_pair = tensor_size == 2 and own_rows % SEQ == 0
    part_count = 2 if by_pair else 1

    def start_rows(own):
        if by_pair:
            return exchange(own, "tensor", 2, 1)
        return lax.all_gather(own, "tensor", axis=0, tiled=True)

    def all_rows(own, got):
        return [own, got] if by_pair else [got]

    def start_sum(parts):
        if by_pair:
            return exchange(parts[1], "tensor", 2, 1)
        return lax.psum_scatter(parts[0], "tensor", scatter_dimension=0, tiled=True)

    def add_sum(parts, got, base=0.0):
        total = base + got.astype(F32)
        return total + parts[0].astype(F32) if by_pair else total

    tables = rope_tables(width)
    gains = gain_query[None, :], gain_keys[None, :]
    places = relative_places(dp_size)
    z_flips = z_bits(dp_size)
    x_flip, z_flip, z_first = 2, z_flips[-1], z_flips[:-1]

    def gather_start(packed, steps):
        first = max(1, steps // 2)
        cuts = [(0, first), (first, steps - first)] if steps > 1 else [(0, 1)]
        unit = packed.shape[1] // steps
        orders = [*z_first, z_flip, x_flip, 1], [*z_first, x_flip, z_flip, 1]
        return cuts, [
            BlockGather(dp_size, packed[:, start * unit : (start + count) * unit], flips)
            for (start, count), flips in zip(cuts, orders)
        ]

    attn_cuts, attn_gathers = gather_start(pack([w_query, key_weight, value_weight, w_output.T], heads), heads)
    inputs_f = inputs.astype(F32)
    unit_in, scale_in = unit_rows(inputs_f)
    normed_own = (unit_in * gain_attn).astype(BF16)
    for gather in attn_gathers:
        gather.start()
    grad_t = turn(places, [grad_out], 0, part_count) if by_pair else ()
    normed_t = turn(places, [normed_own], 0, part_count) if by_pair else ()
    half = own_rows // 2
    grad_half = start_rows(grad_out[:half]) if by_pair else start_rows(grad_out)
    grad_half, packed, *turned = arrive(
        attn_gathers, grad_half, pack([w_gate, w_up, w_down.T], steps), *grad_t, *normed_t
    )
    grad_t, normed_t = turned[:1], turned[1:]

    mlp_cuts, mlp_gathers = gather_start(packed, steps)
    while attn_gathers[0].done < len(attn_gathers[0].flips) - 2:
        for gather in attn_gathers:
            gather.join()
            gather.start()
        arrive(attn_gathers)
    for gather in attn_gathers:
        gather.join()
        gather.start()
    for gather in mlp_gathers:
        gather.start()
    normed_got = start_rows(normed_own)
    (normed_got,) = arrive([*attn_gathers, *mlp_gathers], normed_got)
    normed = all_rows(normed_own, normed_got)
    for gather in attn_gathers:
        gather.join()
        gather.start()
    arrive(attn_gathers)
    attn_chunks = [gather.chunk() for gather in attn_gathers]

    def grow_mlp():
        sent = []
        if mlp_gathers[0].done < len(mlp_gathers[0].flips):
            for gather in mlp_gathers:
                gather.join()
                gather.start()
                sent.append(gather.held)
        return sent

    parts, row_sums, kept = [None] * part_count, [None] * part_count, ()
    grad_rest = start_rows(grad_out[half:]) if by_pair else None
    for index in reversed(range(part_count)):
        after = grow_mlp()
        parts[index], row_sums[index], *kept = attend(
            normed[index], attn_cuts, attn_chunks, tables, *gains, group, width, index, part_count, after, kept
        )
        if index == part_count - 1:
            if by_pair:
                parts[index], grad_rest = arrive(mlp_gathers, parts[index], grad_rest)
            else:
                (parts[index],) = arrive(mlp_gathers, parts[index])
            part_got = start_sum(parts)
    parts[0], part_got = arrive(mlp_gathers, parts[0], part_got)
    kept, head_out = kept
    while mlp_gathers[0].done < len(mlp_gathers[0].flips):
        grow_mlp()
        arrive(mlp_gathers)
    mlp_chunks = [gather.chunk() for gather in mlp_gathers]
    grad_rows = [grad_out, jnp.concatenate([grad_half, grad_rest], axis=0)] if by_pair else [grad_half]
    middle = add_sum(parts, part_got, inputs_f)
    unit_mid, scale_mid = unit_rows(middle)
    normed_own = (unit_mid * gain_mlp).astype(BF16)
    normed_got = start_rows(normed_own)

    def run_mlp(index, array, after, into):
        return mlp(
            array, grad_rows[index], gain_mlp[None, :], mlp_cuts, mlp_chunks, index, part_count, after, into
        )

    if by_pair:
        ffn, dx, dgain, *kept_mlp = run_mlp(0, normed_own, [normed_own], ())
        grad_t = turn(places, grad_rows[1:], 1, part_count, [dx], grad_t)
        normed_t = turn(places, normed[1:], 1, part_count, grad_t, normed_t)
        dx, normed_got, *turned = sync(dx, normed_got, *grad_t, *normed_t)
        grad_t, normed_t = turned[:1], turned[1:]
        ffn_parts, dx_parts, dgain_mlp = [ffn], [dx], dgain[0]
        ffn, dx, dgain, *kept_mlp = run_mlp(1, normed_got, [dx], kept_mlp)
        ffn_parts.append(ffn)
        dx_parts.append(dx)
        dgain_mlp = dgain_mlp + dgain[0]
        after = [dx]
    else:
        grad_t = turn(places, grad_rows, 0, 1)
        normed_t = turn(places, normed, 0, 1)
        ffn, dx, dgain, *kept_mlp = run_mlp(0, normed_got, (), ())
        ffn_parts, dx_parts, dgain_mlp = [ffn], [dx], dgain[0]
        after = [dx]
    normed_mlp_t = turn(places, all_rows(normed_own, normed_got), 0, part_count, after, flops=10**9)

    dx_got = start_sum(dx_parts)
    orders = [x_flip, z_flip, *z_first], [z_flip, x_flip, *z_first]

    def mlp_weight_grads(index, after):
        keep, send, token = weight_grads(
            *normed_mlp_t, *grad_t, *kept_mlp, steps, *mlp_cuts[index], after, index > 0
        )
        return token, BlockSum(dp_size, keep, send, orders[index])

    keep, block_sum = mlp_weight_grads(0, after)
    mlp_sums = [block_sum]
    keep, dx_got = sync(keep, dx_got)
    grad_middle = grad_out.astype(F32) + norm_back(unit_mid, scale_mid, add_sum(dx_parts, dx_got) * gain_mlp)
    attended_own = grad_middle.astype(BF16)
    attended_got = start_rows(attended_own)
    after = [attended_own]
    if len(mlp_cuts) > 1:
        keep, block_sum = mlp_weight_grads(1, after)
        mlp_sums.append(block_sum)
        after = [keep]
    attended_t = turn(places, [attended_own], 0, part_count, after) if by_pair else ()
    keep, *attended_t = arrive(mlp_sums, keep, *attended_t)
    after = [keep, *attended_t, *[block_sum.halve() for block_sum in mlp_sums]]

    dx_parts, dproj, dgain_heads = [], (), 0.0
    if not by_pair:
        (attended_got,) = sync(attended_got)
    for index in range(part_count):
        grad = attended_own if by_pair and index == 0 else attended_got
        dx, dgain, *dproj = attend_back(
            grad, kept, head_out, row_sums[index], attn_cuts, attn_chunks, tables, *gains, group, width, index, part_count, after, dproj
        )
        dgain_heads = dgain_heads + dgain
        if by_pair and index == 0:
            dx, attended_got, ffn_parts[1] = arrive(mlp_sums, dx, attended_got, ffn_parts[1])
            ffn_first = start_rows(ffn_parts[1][:half])
        elif by_pair:
            dx, ffn_first = arrive(mlp_sums, dx, ffn_first)
            ffn_rest = start_rows(ffn_parts[1][half:])
        else:
            (dx,) = arrive(mlp_sums, dx)
            ffn_rest = start_sum(ffn_parts)
        dx_parts.append(dx)
        after = [block_sum.halve() for block_sum in mlp_sums]
    dx_got = start_sum(dx_parts)
    if by_pair:
        attended_t = turn(places, [attended_got], 1, part_count, after, attended_t, 10**9)
    else:
        attended_t = turn(places, [attended_got], 0, 1, after)
    dgain_attn = sum(
        jnp.sum(array.astype(F32) * dx.astype(F32), axis=0) for array, dx in zip(normed, dx_parts)
    ) / gain_attn
    sums = jnp.concatenate([dgain_attn, dgain_mlp, dgain_heads[0], dgain_heads[1]]).reshape(-1, 128)
    hops = [("dp", dp_size, 1 << bit) for bit in range(dp_size.bit_length() - 1)]
    hops += [("tensor", tensor_size, 1 << bit) for bit in range(tensor_size.bit_length() - 1)]
    attn_sums, after = [], [*after, sums]
    for index, cut in enumerate(attn_cuts):
        sums_got = exchange(sums, *hops.pop(0)) if index == 0 else None
        keep, send, token = weight_grads(*normed_t, *attended_t, *dproj, head_out, heads, *cut, after, index > 0)
        attn_sums.append(BlockSum(dp_size, keep, send, orders[index]))
        if index == 0:
            token, sums_got, ffn_rest = arrive(mlp_sums[:1], token, sums_got, ffn_rest)
            sums = sums + sums_got
        after = [token]
    ffn_got = jnp.concatenate([ffn_first, ffn_rest], axis=0) if by_pair else ffn_rest

    sums_got = exchange(sums, *hops.pop(0))
    (sums_got,) = arrive(attn_sums, sums_got)
    sums = sums + sums_got
    sent = [block_sum.halve() for block_sum in attn_sums]
    sums_got = exchange(sums, *hops.pop(0))
    (sums_got,) = arrive(attn_sums, sums_got)
    sums = sums + sums_got
    sent = [block_sum.halve() for block_sum in attn_sums]
    dx_got, *_ = sync(dx_got, *sent)
    grad_normed = add_sum(dx_parts, dx_got)
    grad_inputs = (grad_middle + norm_back(unit_in, scale_in, grad_normed * gain_attn)).astype(BF16)
    sums_got = exchange(sums, *hops.pop(0))
    (sums_got,) = arrive([*attn_sums, *mlp_sums[1:]], sums_got)
    sums = sums + sums_got
    while any(block_sum.flips for block_sum in attn_sums):
        for block_sum in attn_sums:
            block_sum.halve()
    for hop in hops:
        sums = sums + exchange(sums, *hop)
    sums = sums.reshape(-1)
    layer_out = add_sum(ffn_parts, ffn_got, middle).astype(BF16)
    while any(block_sum.flips for block_sum in mlp_sums):
        for block_sum in mlp_sums:
            block_sum.halve()
    mlp_parts = jnp.concatenate([block_sum.finish() for block_sum in mlp_sums], axis=1)
    attn_parts = jnp.concatenate([block_sum.finish() for block_sum in attn_sums], axis=1)
    query_part, keys_part, values_part, output_part = unpack(
        attn_parts, heads, [w_query.shape[1], key_weight.shape[1], value_weight.shape[1], w_output.shape[0]]
    )
    gate_part, up_part, down_part = unpack(mlp_parts, steps, [hidden, hidden, hidden])
    return (
        layer_out,
        grad_inputs,
        query_part,
        keys_part,
        values_part,
        output_part.T,
        gate_part,
        up_part,
        down_part.T,
        sums[:model],
        sums[model : 2 * model],
        sums[2 * model : 2 * model + width],
        sums[2 * model + width :],
    )


def solution(mesh):
    rows = P(("dp", "tensor"), None)
    wide, tall = P("dp", "tensor"), P("tensor", "dp")
    return jax.shard_map(
        functools.partial(body, mesh.shape["dp"], mesh.shape["tensor"]),
        mesh=mesh,
        in_specs=(rows, rows, wide, wide, wide, tall, wide, wide, tall, P(), P(), P(), P()),
        out_specs=(rows, rows, wide, wide, wide, tall, wide, wide, tall, P(), P(), P(), P()),
        check_vma=False,
    )
```

```python
import functools

import jax
import jax.numpy as jnp
import numpy as np
from jax import lax
from jax.experimental import pallas as pl
from jax.experimental.pallas import tpu as pltpu
from jax.sharding import PartitionSpec as P

SEQ = 512
EPSILON = 1e-06
THETA = 1000000.0
F32 = jnp.float32
BF16 = jnp.bfloat16
VMEM_LIMIT = 56 * 1024 * 1024
QUERY_TILE = 256
KEY_TILE = 128


def dot(left, right):
    return lax.dot_general(left, right, (((1,), (0,)), ((), ())), preferred_element_type=F32)


def dot_t(left, right):
    return lax.dot_general(left, right, (((1,), (1,)), ((), ())), preferred_element_type=F32)


def whole(array):
    dims = array.shape
    return pl.BlockSpec(dims, lambda *_: (0,) * len(dims))


def columns(array, count, first=0):
    return pl.BlockSpec((array.shape[0], array.shape[1] // count), lambda j: (0, first + j))


def kernel_call(kernel, name, grid, inputs, outputs, scratch, flops, after=(), into=(), into_index=0):
    after = [*into, *after]
    known = len(inputs)

    def run(*refs):
        kernel(*refs[:known], *refs[known + len(after) :])

    moved = sum(array.size * array.dtype.itemsize for array, _ in inputs)
    return pl.pallas_call(
        run,
        grid=grid,
        in_specs=[spec for _, spec in inputs] + [pl.BlockSpec(memory_space=pl.ANY)] * len(after),
        out_specs=[spec for _, _, spec in outputs],
        out_shape=[jax.ShapeDtypeStruct(shape, dtype) for shape, dtype, _ in outputs],
        scratch_shapes=scratch,
        input_output_aliases={known + index: into_index + index for index in range(len(into))},
        compiler_params=pltpu.CompilerParams(vmem_limit_bytes=VMEM_LIMIT),
        cost_estimate=pl.CostEstimate(flops=64 * flops, bytes_accessed=64 * moved if flops else 1, transcendentals=0),
        name=name,
    )(*[array for array, _ in inputs], *after)


def sync(*arrays):
    spec = pl.BlockSpec(memory_space=pl.ANY)
    return kernel_call(
        lambda *_: None, "sync", (), [], [(array.shape, array.dtype, spec) for array in arrays], [], 0, (), arrays
    )


def rope_tables(width):
    half = width // 2
    places = np.arange(SEQ, dtype=np.float32)
    inverse = (THETA ** (-2.0 * np.arange(half, dtype=np.float32) / width)).astype(np.float32)
    angles = places[:, None] * inverse[None, :]
    cosine = np.concatenate([np.cos(angles), np.cos(angles)], axis=-1)
    sine = np.concatenate([-np.sin(angles), np.sin(angles)], axis=-1)
    return cosine.astype(np.float32), sine.astype(np.float32)


def rope(values, cosine, sine):
    half = values.shape[-1] // 2
    return values * cosine + pltpu.roll(values, half, 1) * sine


def rope_back(values, cosine, sine):
    half = values.shape[-1] // 2
    return values * cosine + pltpu.roll(values * sine, half, 1)


def score_tiles():
    for query in range(0, SEQ, QUERY_TILE):
        for key in range(0, query + QUERY_TILE, KEY_TILE):
            yield slice(key, key + KEY_TILE), slice(query, query + QUERY_TILE)


def exponents_t(keys_rot, query_rot, factor, keys, queries):
    result = jnp.exp2(dot_t(keys_rot, query_rot) * factor)
    if keys.stop - 1 <= queries.start:
        return result
    key_place = lax.broadcasted_iota(jnp.int32, result.shape, 0) + keys.start
    query_place = lax.broadcasted_iota(jnp.int32, result.shape, 1) + queries.start
    return jnp.where(key_place <= query_place, result, 0.0)


def load_weights(cuts, chunks, weight_ref):
    step = pl.program_id(0)
    for index, (first, count) in enumerate(cuts):
        places_ref, *halves = chunks[3 * index : 3 * index + 3]

        @pl.when((step >= first) & (step < first + count))
        def _():
            blocks = places_ref.shape[0]
            block = weight_ref.shape[0] // blocks
            for position in range(blocks):
                half, inner = halves[2 * position // blocks], position % (blocks // 2)
                place = pl.ds(pl.multiple_of(places_ref[position] * block, block), block)
                weight_ref[place, :] = half[inner * block : (inner + 1) * block, :]


def weight_inputs(cuts, chunks):
    inputs = []
    for (first, count), (places, *halves) in zip(cuts, chunks):
        inputs.append((places, pl.BlockSpec(memory_space=pltpu.SMEM)))
        for half in halves:
            spec = pl.BlockSpec(
                (half.shape[0], half.shape[1] // count),
                lambda j, first=first, count=count: (0, jnp.clip(j - first, 0, count - 1)),
            )
            inputs.append((half, spec))
    return inputs


def attend_kernel(group, width, cuts, normed_ref, cos_ref, sin_ref, gain_q_ref, gain_k_ref, *refs):
    chunks, (part_ref, sums_ref, kept_ref, out_ref, total, weight_ref) = refs[: 3 * len(cuts)], refs[3 * len(cuts) :]
    step = pl.program_id(0)
    load_weights(cuts, chunks, weight_ref)
    rows = normed_ref.shape[0]
    wide = group * width
    factor = float(width**-0.5 * np.log2(np.e))
    proj = dot(normed_ref[...], weight_ref[:, : wide + 2 * width])
    kept_ref[:, : wide + width] = proj[:, : wide + width].astype(BF16)
    values = proj[:, wide + width :].astype(BF16)
    kept_ref[:, 2 * (wide + width) :] = values
    for seq in range(rows // SEQ):
        place = slice(seq * SEQ, (seq + 1) * SEQ)
        rotated = []
        for head in range(group + 1):
            raw = proj[place, head * width : (head + 1) * width]
            scale = lax.rsqrt(jnp.mean(raw * raw, axis=-1, keepdims=True) + EPSILON)
            gain = gain_q_ref[...] if head < group else gain_k_ref[...]
            turned = rope(raw * scale * gain, cos_ref[...], sin_ref[...]).astype(BF16)
            kept_ref[place, wide + width + head * width : wide + width + (head + 1) * width] = turned
            rotated.append(turned)
        values_t = values[place].T
        for head in range(group):
            out_t, sums = {}, {}
            for keys, queries in score_tiles():
                exponents = exponents_t(rotated[group][keys], rotated[head][queries], factor, keys, queries)
                start = queries.start
                sums[start] = sums.get(start, 0.0) + jnp.sum(exponents, axis=0, keepdims=True)
                out_t[start] = out_t.get(start, 0.0) + dot(values_t[:, keys], exponents.astype(BF16))
            for start in out_t:
                scale = 1.0 / sums[start]
                spot = slice(seq * SEQ + start, seq * SEQ + start + QUERY_TILE)
                sums_ref[head : head + 1, spot] = scale
                out_ref[spot, head * width : (head + 1) * width] = (out_t[start] * scale).T.astype(BF16)
    out = dot_t(out_ref[...], weight_ref[:, wide + 2 * width :])

    @pl.when(step == 0)
    def _():
        total[...] = out

    @pl.when(step > 0)
    def _():
        total[...] += out

    @pl.when(step == pl.num_programs(0) - 1)
    def _():
        part_ref[...] = total[...].astype(BF16)


def part_rows(rows, width, steps, part, parts):
    return (parts * rows, width), BF16, pl.BlockSpec((rows, width // steps), lambda j: (part, j))


def attend(normed, cuts, chunks, tables, gain_q, gain_k, group, width, part, parts, after=(), into=()):
    rows, model = normed.shape
    heads = sum(count for _, count in cuts)
    block = (2 * group + 2) * width
    return kernel_call(
        functools.partial(attend_kernel, group, width, cuts),
        "attend",
        (heads,),
        [(array, whole(array)) for array in (normed, *tables, gain_q, gain_k)] + weight_inputs(cuts, chunks),
        [
            (normed.shape, BF16, whole(normed)),
            ((8 * heads, rows), F32, pl.BlockSpec((8, rows), lambda j: (j, 0))),
            part_rows(rows, heads * (2 * group + 3) * width, heads, part, parts),
            part_rows(rows, heads * group * width, heads, part, parts),
        ],
        [pltpu.VMEM((rows, model), F32), pltpu.VMEM((model, block), BF16)],
        heads * (2 * rows * model * block + 4 * rows * SEQ * group * width),
        after,
        into,
        2,
    )


def turn_kernel(places_ref, *refs):
    target_ref = refs[-1]
    count = places_ref.shape[0]
    block = target_ref.shape[0] // count
    together = max(1, min(count, 128 // block))
    begin = 0
    for source_ref in refs[:-1]:
        rows = source_ref.shape[0]
        for first in range(0, count, together):
            turned = source_ref[:, first * block : (first + together) * block].T
            for index in range(together):
                place = pl.ds(pl.multiple_of(places_ref[first + index] * block, block), block)
                target_ref[place, begin : begin + rows] = turned[index * block : (index + 1) * block]
        begin += rows


def turn(places, sources, part, parts, after=(), into=(), flops=0):
    rows, model = sources[0].shape
    width = rows * len(sources)
    return kernel_call(
        turn_kernel,
        "turn",
        (1,),
        [(places, pl.BlockSpec(memory_space=pltpu.SMEM))] + [(source, whole(source)) for source in sources],
        [((model, rows * parts), BF16, pl.BlockSpec((model, width), lambda j: (0, part // len(sources))))],
        [],
        flops,
        after,
        into,
    )


def mlp_kernel(cuts, normed_ref, grad_ref, gain_ref, *refs):
    chunks = refs[: 3 * len(cuts)]
    out_ref, dx_ref, dgain_ref, both_ref, hidden_ref, out_total, dx_total, weight_ref = refs[3 * len(cuts) :]
    step = pl.program_id(0)
    units = weight_ref.shape[1] // 3
    load_weights(cuts, chunks, weight_ref)

    @pl.when(step == 0)
    def _():
        out_total[...] = jnp.zeros_like(out_total)
        dx_total[...] = jnp.zeros_like(dx_total)

    both = dot(normed_ref[...], weight_ref[:, : 2 * units])
    gate, up = both[:, :units], both[:, units:]
    sig = 1.0 / (1.0 + jnp.exp(-gate))
    silu = gate * sig
    hidden = (silu * up).astype(BF16)
    grad_hidden = dot(grad_ref[...], weight_ref[:, 2 * units :])
    both_ref[:, :units] = (grad_hidden * up * (sig + silu * (1.0 - sig))).astype(BF16)
    both_ref[:, units:] = (grad_hidden * silu).astype(BF16)
    hidden_ref[...] = hidden
    out_total[...] += dot_t(hidden, weight_ref[:, 2 * units :])
    dx_total[...] += dot_t(both_ref[...], weight_ref[:, : 2 * units])

    @pl.when(step == pl.num_programs(0) - 1)
    def _():
        out_ref[...] = out_total[...].astype(BF16)
        dx_ref[...] = dx_total[...].astype(BF16)
        dgain_ref[...] = (
            jnp.sum(normed_ref[...].astype(F32) * dx_total[...], axis=0, keepdims=True) / gain_ref[...]
        )


def mlp(normed, grad_rows, gain, cuts, chunks, part, parts, after=(), into=()):
    rows, model = normed.shape
    steps = sum(count for _, count in cuts)
    units = chunks[0][1].shape[1] // cuts[0][1] // 3
    return kernel_call(
        functools.partial(mlp_kernel, cuts),
        "mlp",
        (steps,),
        [(array, whole(array)) for array in (normed, grad_rows, gain)] + weight_inputs(cuts, chunks),
        [
            (normed.shape, BF16, whole(normed)),
            (normed.shape, BF16, whole(normed)),
            (gain.shape, F32, whole(gain)),
            part_rows(rows, steps * 2 * units, steps, part, parts),
            part_rows(rows, steps * units, steps, part, parts),
        ],
        [pltpu.VMEM((rows, model), F32), pltpu.VMEM((rows, model), F32), pltpu.VMEM((model, 3 * units), BF16)],
        12 * rows * model * steps * units,
        after,
        into,
        3,
    )


def weight_grads_kernel(in_t, out_t, into, outof, *halves):
    wide = into.shape[1]
    half = in_t.shape[0] // 2
    *halves, token_ref = halves
    token_ref[...] = jnp.zeros_like(token_ref)
    for ref, place in zip(halves, (slice(0, half), slice(half, 2 * half))):
        ref[:, :wide] = dot(in_t[place, :], into[...]).astype(BF16)
        ref[:, wide:] = dot(out_t[place, :], outof[...]).astype(BF16)


def weight_grads(in_t, out_t, into, outof, steps, first, count, after=(), hides=True):
    model, rows = in_t.shape
    token = jax.ShapeDtypeStruct((8, 128), F32)
    target = jax.ShapeDtypeStruct((model // 2, count * (into.shape[1] + outof.shape[1]) // steps), BF16)
    return kernel_call(
        weight_grads_kernel,
        "weight_grads",
        (count,),
        [(in_t, whole(in_t)), (out_t, whole(out_t))]
        + [(array, columns(array, steps, first)) for array in (into, outof)],
        [(target.shape, BF16, columns(target, count))] * 2 + [(token.shape, F32, whole(token))],
        [],
        4 * rows * target.size if hides else 0,
        after,
    )


def attend_back_kernel(
    group, width, cuts, grad_ref, kept, out_ref, sums_ref, cos_ref, sin_ref, gain_q_ref, gain_k_ref, *refs
):
    chunks = refs[: 3 * len(cuts)]
    dx_ref, dgain_ref, dproj, total, weight_ref = refs[3 * len(cuts) :]
    step = pl.program_id(0)
    load_weights(cuts, chunks, weight_ref)
    wide = group * width
    scaling = float(width**-0.5)
    factor = float(width**-0.5 * np.log2(np.e))
    rot = wide + width
    base = 2 * rot

    @pl.when(step == 0)
    def _():
        total[...] = jnp.zeros_like(total)
        dgain_ref[...] = jnp.zeros_like(dgain_ref)

    def head_back(place, head, cotangent):
        gain = gain_q_ref[...] if head < group else gain_k_ref[...]
        raw = kept[place, head * width : (head + 1) * width].astype(F32)
        scale = lax.rsqrt(jnp.mean(raw * raw, axis=-1, keepdims=True) + EPSILON)
        unit = raw * scale
        cot = rope_back(cotangent * scaling, cos_ref[...], sin_ref[...])
        row = 0 if head < group else 1
        dgain_ref[row : row + 1, :] += jnp.sum(cot * unit, axis=0, keepdims=True)
        cot = cot * gain
        result = scale * (cot - unit * jnp.mean(unit * cot, axis=-1, keepdims=True))
        dproj[place, head * width : (head + 1) * width] = result.astype(BF16)

    grad_heads = dot(grad_ref[...], weight_ref[:, wide + 2 * width :]).astype(BF16)
    for seq in range(grad_heads.shape[0] // SEQ):
        place = slice(seq * SEQ, (seq + 1) * SEQ)
        keys_rot = kept[place, rot + wide : rot + wide + width]
        keys_t = keys_rot.T
        values = kept[place, base : base + width]
        dkeys, dvalues = [{key: 0.0 for key in range(0, SEQ, KEY_TILE)} for _ in range(2)]
        for head in range(group):
            query_rot = kept[place, rot + head * width : rot + (head + 1) * width]
            grad_head = grad_heads[place, head * width : (head + 1) * width]
            weighted = grad_head.astype(F32) * out_ref[place, head * width : (head + 1) * width].astype(F32)
            inner = jnp.sum(weighted.T, axis=0, keepdims=True)
            scale = sums_ref[head : head + 1, place]
            dqueries = {}
            for keys, queries in score_tiles():
                exponents = exponents_t(keys_rot[keys], query_rot[queries], factor, keys, queries)
                probs = exponents * scale[:, queries]
                dprobs = dot_t(values[keys], grad_head[queries])
                dscores = (probs * (dprobs - inner[:, queries])).astype(BF16)
                dvalues[keys.start] += dot(probs.astype(BF16), grad_head[queries])
                dkeys[keys.start] += dot(dscores, query_rot[queries])
                start = queries.start
                dqueries[start] = dqueries.get(start, 0.0) + dot(keys_t[:, keys], dscores)
            head_back(place, head, jnp.concatenate([dqueries[start].T for start in dqueries], axis=0))
        dkeys = jnp.concatenate(list(dkeys.values()), axis=0)
        dvalues = jnp.concatenate(list(dvalues.values()), axis=0)
        head_back(place, group, dkeys)
        dproj[place, wide + width :] = dvalues.astype(BF16)
    total[...] += dot_t(dproj[...], weight_ref[:, : wide + 2 * width])

    @pl.when(step == pl.num_programs(0) - 1)
    def _():
        dx_ref[...] = total[...].astype(BF16)


def attend_back(grad, kept, head_out, sums, cuts, chunks, tables, gain_q, gain_k, group, width, part, parts, after=(), into=()):
    rows, model = grad.shape
    heads = sum(count for _, count in cuts)
    block = (2 * group + 2) * width
    return kernel_call(
        functools.partial(attend_back_kernel, group, width, cuts),
        "attend_back",
        (heads,),
        [
            (grad, whole(grad)),
            (kept, pl.BlockSpec((rows, kept.shape[1] // heads), lambda j: (part, j))),
            (head_out, pl.BlockSpec((rows, head_out.shape[1] // heads), lambda j: (part, j))),
            (sums, pl.BlockSpec((8, rows), lambda j: (j, 0))),
            *[(array, whole(array)) for array in (*tables, gain_q, gain_k)],
            *weight_inputs(cuts, chunks),
        ],
        [
            (grad.shape, BF16, whole(grad)),
            ((8, width), F32, pl.BlockSpec((8, width), lambda j: (0, 0))),
            part_rows(rows, heads * (group + 2) * width, heads, part, parts),
        ],
        [pltpu.VMEM((rows, model), F32), pltpu.VMEM((model, block), BF16)],
        heads * (2 * rows * model * block + 10 * rows * SEQ * group * width),
        after,
        into,
        2,
    )


def unit_rows(values):
    scale = lax.rsqrt(jnp.mean(values * values, axis=-1, keepdims=True) + EPSILON)
    return values * scale, scale


def norm_back(unit, scale, cotangent):
    return scale * (cotangent - unit * jnp.mean(unit * cotangent, axis=-1, keepdims=True))


def pack(parts, pieces):
    return jnp.concatenate(
        [
            part[:, index * part.shape[1] // pieces : (index + 1) * part.shape[1] // pieces]
            for index in range(pieces)
            for part in parts
        ],
        axis=1,
    )


def unpack(packed, pieces, widths):
    unit = packed.shape[1] // pieces
    ends = np.cumsum([width // pieces for width in widths])
    return [
        jnp.concatenate(
            [
                packed[:, index * unit + end - width // pieces : index * unit + end]
                for index in range(pieces)
            ],
            axis=1,
        )
        for end, width in zip(ends, widths)
    ]


def relative_places(size):
    relative = jnp.arange(size, dtype=jnp.int32) ^ lax.axis_index("dp")
    layers = size // 4
    return (relative & 1) * (2 * layers) + ((relative >> 1) & 1) * layers + (relative >> 2)


def exchange(array, axis, size, flip):
    return lax.ppermute(array, axis, [(index, index ^ flip) for index in range(size)])


def z_bits(size):
    return [4 << bit for bit in reversed(range((size // 4).bit_length() - 1))]


class BlockGather:
    def __init__(self, size, block, flips):
        self.size, self.flips = size, list(flips)
        self.held, self.done, self.got = block, 0, None

    def start(self):
        self.got = exchange(self.held, "dp", self.size, self.flips[self.done])
        self.done += 1

    def join(self):
        self.held = jnp.concatenate([self.held, self.got], axis=0)

    def chunk(self):
        position = jnp.arange(self.size, dtype=jnp.int32)
        place = lax.axis_index("dp") ^ sum(
            ((position >> bit) & 1) * flip for bit, flip in enumerate(self.flips)
        )
        return place, self.held, self.got


class BlockSum:
    def __init__(self, size, keep, send, flips):
        self.size, self.flips = size, list(flips)
        self.bits = [2, *z_bits(size)]
        self.left = list(self.bits)
        self.shape = (2,) * len(self.bits) + (-1, keep.shape[1])
        self.terms = [(keep.reshape(self.shape), self.bits)]
        self.got = exchange(send, "dp", size, 1)

    def part(self, flip=None):
        total = 0.0
        for array, bits in self.terms:
            start = [int(bit == flip) for bit in bits] + [0, 0]
            stop = [
                int(bit == flip) + 1 if bit == flip or bit not in self.left else 2 for bit in bits
            ] + list(array.shape[-2:])
            piece = lax.slice(array, start, stop)
            total = total + piece.reshape((2,) * (len(self.left) - (flip is not None)) + piece.shape[-2:]).astype(F32)
        return total

    def take(self):
        if len(self.terms) == 1:
            self.got = self.got.reshape(self.shape)
        self.terms.append((self.got, list(self.left)))

    def halve(self):
        self.take()
        flip = self.flips.pop(0)
        sent = self.part(flip).astype(BF16)
        self.left.remove(flip)
        self.got = exchange(sent, "dp", self.size, flip)
        return sent

    def finish(self):
        self.take()
        return self.part()


def arrive(movers, *others):
    results = sync(*[mover.got for mover in movers], *others)
    for mover, got in zip(movers, results):
        mover.got = got
    return results[len(movers) :]


def body(
    dp_size,
    tensor_size,
    inputs,
    grad_out,
    w_query,
    key_weight,
    value_weight,
    w_output,
    w_gate,
    w_up,
    w_down,
    gain_attn,
    gain_mlp,
    gain_query,
    gain_keys,
):
    own_rows, model = inputs.shape
    width = gain_query.shape[0]
    heads = key_weight.shape[1] // width
    group = w_query.shape[1] // key_weight.shape[1]
    hidden = w_gate.shape[1]
    steps = max(1, hidden // 256)
    by_pair = tensor_size == 2 and own_rows % SEQ == 0
    part_count = 2 if by_pair else 1

    def start_rows(own):
        if by_pair:
            return exchange(own, "tensor", 2, 1)
        return lax.all_gather(own, "tensor", axis=0, tiled=True)

    def all_rows(own, got):
        return [own, got] if by_pair else [got]

    def start_sum(parts):
        if by_pair:
            return exchange(parts[1], "tensor", 2, 1)
        return lax.psum_scatter(parts[0], "tensor", scatter_dimension=0, tiled=True)

    def add_sum(parts, got, base=0.0):
        total = base + got.astype(F32)
        return total + parts[0].astype(F32) if by_pair else total

    tables = rope_tables(width)
    gains = gain_query[None, :], gain_keys[None, :]
    places = relative_places(dp_size)
    z_flips = z_bits(dp_size)
    x_flip, z_flip, z_first = 2, z_flips[-1], z_flips[:-1]

    def gather_start(packed, steps):
        first = max(1, steps // 2)
        cuts = [(0, first), (first, steps - first)] if steps > 1 else [(0, 1)]
        unit = packed.shape[1] // steps
        orders = [*z_first, z_flip, x_flip, 1], [*z_first, x_flip, z_flip, 1]
        return cuts, [
            BlockGather(dp_size, packed[:, start * unit : (start + count) * unit], flips)
            for (start, count), flips in zip(cuts, orders)
        ]

    attn_cuts, attn_gathers = gather_start(pack([w_query, key_weight, value_weight, w_output.T], heads), heads)
    inputs_f = inputs.astype(F32)
    unit_in, scale_in = unit_rows(inputs_f)
    normed_own = (unit_in * gain_attn).astype(BF16)
    for gather in attn_gathers:
        gather.start()
    grad_t = turn(places, [grad_out], 0, part_count) if by_pair else ()
    normed_t = turn(places, [normed_own], 0, part_count) if by_pair else ()
    half = own_rows // 2
    grad_half = start_rows(grad_out[:half]) if by_pair else start_rows(grad_out)
    grad_half, packed, *turned = arrive(
        attn_gathers, grad_half, pack([w_gate, w_up, w_down.T], steps), *grad_t, *normed_t
    )
    grad_t, normed_t = turned[:1], turned[1:]

    mlp_cuts, mlp_gathers = gather_start(packed, steps)
    while attn_gathers[0].done < len(attn_gathers[0].flips) - 2:
        for gather in attn_gathers:
            gather.join()
            gather.start()
        arrive(attn_gathers)
    for gather in attn_gathers:
        gather.join()
        gather.start()
    for gather in mlp_gathers:
        gather.start()
    normed_got = start_rows(normed_own)
    (normed_got,) = arrive([*attn_gathers, *mlp_gathers], normed_got)
    normed = all_rows(normed_own, normed_got)
    for gather in attn_gathers:
        gather.join()
        gather.start()
    arrive(attn_gathers)
    attn_chunks = [gather.chunk() for gather in attn_gathers]

    def grow_mlp():
        sent = []
        if mlp_gathers[0].done < len(mlp_gathers[0].flips):
            for gather in mlp_gathers:
                gather.join()
                gather.start()
                sent.append(gather.held)
        return sent

    parts, row_sums, kept = [None] * part_count, [None] * part_count, ()
    grad_rest = start_rows(grad_out[half:]) if by_pair else None
    for index in reversed(range(part_count)):
        after = grow_mlp()
        parts[index], row_sums[index], *kept = attend(
            normed[index], attn_cuts, attn_chunks, tables, *gains, group, width, index, part_count, after, kept
        )
        if index == part_count - 1:
            if by_pair:
                parts[index], grad_rest = arrive(mlp_gathers, parts[index], grad_rest)
            else:
                (parts[index],) = arrive(mlp_gathers, parts[index])
            part_got = start_sum(parts)
    parts[0], part_got = arrive(mlp_gathers, parts[0], part_got)
    kept, head_out = kept
    while mlp_gathers[0].done < len(mlp_gathers[0].flips):
        grow_mlp()
        arrive(mlp_gathers)
    mlp_chunks = [gather.chunk() for gather in mlp_gathers]
    grad_rows = [grad_out, jnp.concatenate([grad_half, grad_rest], axis=0)] if by_pair else [grad_half]
    middle = add_sum(parts, part_got, inputs_f)
    unit_mid, scale_mid = unit_rows(middle)
    normed_own = (unit_mid * gain_mlp).astype(BF16)
    normed_got = start_rows(normed_own)

    def run_mlp(index, array, after, into):
        return mlp(
            array, grad_rows[index], gain_mlp[None, :], mlp_cuts, mlp_chunks, index, part_count, after, into
        )

    if by_pair:
        ffn, dx, dgain, *kept_mlp = run_mlp(0, normed_own, [normed_own], ())
        grad_t = turn(places, grad_rows[1:], 1, part_count, [dx], grad_t)
        normed_t = turn(places, normed[1:], 1, part_count, grad_t, normed_t)
        dx, normed_got, *turned = sync(dx, normed_got, *grad_t, *normed_t)
        grad_t, normed_t = turned[:1], turned[1:]
        ffn_parts, dx_parts, dgain_mlp = [ffn], [dx], dgain[0]
        ffn, dx, dgain, *kept_mlp = run_mlp(1, normed_got, [dx], kept_mlp)
        ffn_parts.append(ffn)
        dx_parts.append(dx)
        dgain_mlp = dgain_mlp + dgain[0]
        after = [dx]
    else:
        grad_t = turn(places, grad_rows, 0, 1)
        normed_t = turn(places, normed, 0, 1)
        ffn, dx, dgain, *kept_mlp = run_mlp(0, normed_got, (), ())
        ffn_parts, dx_parts, dgain_mlp = [ffn], [dx], dgain[0]
        after = [dx]
    normed_mlp_t = turn(places, all_rows(normed_own, normed_got), 0, part_count, after, flops=10**9)

    dx_got = start_sum(dx_parts)
    orders = [x_flip, z_flip, *z_first], [z_flip, x_flip, *z_first]

    def mlp_weight_grads(index, after):
        keep, send, token = weight_grads(
            *normed_mlp_t, *grad_t, *kept_mlp, steps, *mlp_cuts[index], after, index > 0
        )
        return token, BlockSum(dp_size, keep, send, orders[index])

    keep, block_sum = mlp_weight_grads(0, after)
    mlp_sums = [block_sum]
    keep, dx_got = sync(keep, dx_got)
    grad_middle = grad_out.astype(F32) + norm_back(unit_mid, scale_mid, add_sum(dx_parts, dx_got) * gain_mlp)
    attended_own = grad_middle.astype(BF16)
    attended_got = start_rows(attended_own)
    after = [attended_own]
    if len(mlp_cuts) > 1:
        keep, block_sum = mlp_weight_grads(1, after)
        mlp_sums.append(block_sum)
        after = [keep]
    attended_t = turn(places, [attended_own], 0, part_count, after) if by_pair else ()
    keep, *attended_t = arrive(mlp_sums, keep, *attended_t)
    after = [keep, *attended_t, *[block_sum.halve() for block_sum in mlp_sums]]

    dx_parts, dproj, dgain_heads = [], (), 0.0
    if not by_pair:
        (attended_got,) = sync(attended_got)
    for index in range(part_count):
        grad = attended_own if by_pair and index == 0 else attended_got
        dx, dgain, *dproj = attend_back(
            grad, kept, head_out, row_sums[index], attn_cuts, attn_chunks, tables, *gains, group, width, index, part_count, after, dproj
        )
        dgain_heads = dgain_heads + dgain
        if by_pair and index == 0:
            dx, attended_got, ffn_parts[1] = arrive(mlp_sums, dx, attended_got, ffn_parts[1])
            ffn_first = start_rows(ffn_parts[1][:half])
        elif by_pair:
            dx, ffn_first = arrive(mlp_sums, dx, ffn_first)
            ffn_rest = start_rows(ffn_parts[1][half:])
        else:
            (dx,) = arrive(mlp_sums, dx)
            ffn_rest = start_sum(ffn_parts)
        dx_parts.append(dx)
        after = [block_sum.halve() for block_sum in mlp_sums]
    dx_got = start_sum(dx_parts)
    if by_pair:
        attended_t = turn(places, [attended_got], 1, part_count, after, attended_t, 10**9)
    else:
        attended_t = turn(places, [attended_got], 0, 1, after)
    dgain_attn = sum(
        jnp.sum(array.astype(F32) * dx.astype(F32), axis=0) for array, dx in zip(normed, dx_parts)
    ) / gain_attn
    sums = jnp.concatenate([dgain_attn, dgain_mlp, dgain_heads[0], dgain_heads[1]]).reshape(-1, 128)
    hops = [("dp", dp_size, 1 << bit) for bit in range(dp_size.bit_length() - 1)]
    hops += [("tensor", tensor_size, 1 << bit) for bit in range(tensor_size.bit_length() - 1)]
    attn_sums, after = [], [*after, sums]
    for index, cut in enumerate(attn_cuts):
        sums_got = exchange(sums, *hops.pop(0)) if index == 0 else None
        keep, send, token = weight_grads(*normed_t, *attended_t, *dproj, head_out, heads, *cut, after, index > 0)
        attn_sums.append(BlockSum(dp_size, keep, send, orders[index]))
        if index == 0:
            token, sums_got, ffn_rest = arrive(mlp_sums[:1], token, sums_got, ffn_rest)
            sums = sums + sums_got
        after = [token]
    ffn_got = jnp.concatenate([ffn_first, ffn_rest], axis=0) if by_pair else ffn_rest

    sums_got = exchange(sums, *hops.pop(0))
    (sums_got,) = arrive(attn_sums, sums_got)
    sums = sums + sums_got
    sent = [block_sum.halve() for block_sum in attn_sums]
    sums_got = exchange(sums, *hops.pop(0))
    (sums_got,) = arrive(attn_sums, sums_got)
    sums = sums + sums_got
    sent = [block_sum.halve() for block_sum in attn_sums]
    dx_got, *_ = sync(dx_got, *sent)
    grad_normed = add_sum(dx_parts, dx_got)
    grad_inputs = (grad_middle + norm_back(unit_in, scale_in, grad_normed * gain_attn)).astype(BF16)
    sums_got = exchange(sums, *hops.pop(0))
    (sums_got,) = arrive([*attn_sums, *mlp_sums[1:]], sums_got)
    sums = sums + sums_got
    while any(block_sum.flips for block_sum in attn_sums):
        for block_sum in attn_sums:
            block_sum.halve()
    for hop in hops:
        sums = sums + exchange(sums, *hop)
    sums = sums.reshape(-1)
    layer_out = add_sum(ffn_parts, ffn_got, middle).astype(BF16)
    while any(block_sum.flips for block_sum in mlp_sums):
        for block_sum in mlp_sums:
            block_sum.halve()
    mlp_parts = jnp.concatenate([block_sum.finish() for block_sum in mlp_sums], axis=1)
    attn_parts = jnp.concatenate([block_sum.finish() for block_sum in attn_sums], axis=1)
    query_part, keys_part, values_part, output_part = unpack(
        attn_parts, heads, [w_query.shape[1], key_weight.shape[1], value_weight.shape[1], w_output.shape[0]]
    )
    gate_part, up_part, down_part = unpack(mlp_parts, steps, [hidden, hidden, hidden])
    return (
        layer_out,
        grad_inputs,
        query_part,
        keys_part,
        values_part,
        output_part.T,
        gate_part,
        up_part,
        down_part.T,
        sums[:model],
        sums[model : 2 * model],
        sums[2 * model : 2 * model + width],
        sums[2 * model + width :],
    )


def solution(mesh):
    rows = P(("dp", "tensor"), None)
    wide, tall = P("dp", "tensor"), P("tensor", "dp")
    return jax.shard_map(
        functools.partial(body, mesh.shape["dp"], mesh.shape["tensor"]),
        mesh=mesh,
        in_specs=(rows, rows, wide, wide, wide, tall, wide, wide, tall, P(), P(), P(), P()),
        out_specs=(rows, rows, wide, wide, wide, tall, wide, wide, tall, P(), P(), P(), P()),
        check_vma=False,
    )
```
